512 devices in a mesh: vol: 8 (over x, core), chan: 64 (over y, z).
Axes of the slice: x: 4, y: 8, z: 8, core: 2. Of those that a mesh axis runs over, the one named last changes fastest.
Arguments:
- fwd_input: bfloat16 [8, 256, 12288], P('vol', None, 'chan'), may hold values from 0 to 72, as said below
- weight_one: bfloat16 [27, 256, 256], P(None, 'chan'), may hold values from -0.078125 to 0.078125
- gain_one: float32 [256], P('chan'), may hold values from 0.25 to 1.75
- bias_one: float32 [256], P('chan'), may hold values from -0.5 to 0.5
- saved_conv: bfloat16 [8, 256, 12288], P('vol', 'chan'), may hold values from -39 to 39
- cotangent: bfloat16 [8, 256, 12288], P('vol', 'chan'), may hold values from -26 to 26
- saved_input: bfloat16 [8, 256, 12288], P('vol', 'chan'), may hold values from 0 to 72, as said below
- weight_two: bfloat16 [27, 256, 256], P(None, None, 'chan'), may hold values from -0.078125 to 0.078125
- gain_two: float32 [256], P('chan'), may hold values from 0.25 to 1.75
Outputs:
- activation: bfloat16 [8, 256, 12288], P('vol', 'chan')
- input_grad: bfloat16 [8, 256, 12288], P('vol', 'chan')
- weight_grad: float32 [27, 256, 256], P(None, 'vol', 'chan')
- gain_grad: float32 [256], P('chan')
- shift_grad: float32 [256], P('chan')
The draws below stay inside these ranges and needn't reach their ends.
Inputs may be any that keep to these rules, and one draw needn't show every extreme that they name: `fwd_input`: input activations are never negative. `saved_input`: input activations are never negative.
All inputs are finite; a program needn't handle non-finite values.
Results may differ from the reference program's by a relative error of at most 0.02.
Values may be sent and summed in bfloat16 or wider, within the bound.
No kernel may reach another device: no remote copies, remote signals or barrier semaphores. Data moves between devices by JAX's collectives and lax.ppermute only.
A program may use at most 192 MiB of HBM per device.

```python
import math
import jax
import jax.numpy as jnp
from jax import lax

CH = 256
SIDE = 32
DEPTH = 12
NV = 8
P_SIZE = 12288


def volume_ramp(volumes):
    steps = jnp.arange(volumes, dtype=jnp.float32)
    return (1.0 + 2.0 * steps / max(volumes - 1, 1)).reshape(volumes, 1, 1)


def spread_factors(key):
    keys = jax.random.split(key, 2)
    channel_scale = jax.random.uniform(keys[0], (1, CH, 1), jnp.float32, 0.5, 2.0)
    cell_scale = jnp.exp(jax.random.uniform(keys[1], (1, 1, P_SIZE), jnp.float32, math.log(0.3), math.log(3.0)))
    return (channel_scale, cell_scale)


def common_field(key):
    return jnp.clip(jax.random.normal(key, (NV, CH, P_SIZE), jnp.float32), -4.0, 4.0)


def draw_fwd_input(key, part):
    key = jax.random.fold_in(key, 11)
    keys = jax.random.split(key, 2)
    magnitude = jnp.minimum(jnp.abs(jax.random.normal(keys[0], (NV, CH, P_SIZE), jnp.float32)), 4.0)
    channel_scale, cell_scale = spread_factors(keys[1])
    return (magnitude * channel_scale * cell_scale * volume_ramp(NV)).astype(jnp.bfloat16)


def draw_saved_input(key, part):
    key = jax.random.fold_in(key, 12)
    keys = jax.random.split(key, 2)
    magnitude = jnp.minimum(jnp.abs(jax.random.normal(keys[0], (NV, CH, P_SIZE), jnp.float32)), 4.0)
    channel_scale, cell_scale = spread_factors(keys[1])
    return (magnitude * channel_scale * cell_scale * volume_ramp(NV)).astype(jnp.bfloat16)


def draw_saved_conv(key, part):
    shared = common_field(key)
    key = jax.random.fold_in(key, 21)
    keys = jax.random.split(key, 2)
    offsets = jax.random.uniform(keys[0], (1, CH, 1), jnp.float32, -1.0, 1.0)
    cell_scale = jnp.exp(jax.random.uniform(keys[1], (1, 1, P_SIZE), jnp.float32, math.log(0.3), math.log(3.0)))
    return (volume_ramp(NV) * (offsets + shared * cell_scale)).astype(jnp.bfloat16)


def draw_cotangent(key, part):
    shared = common_field(key)
    key = jax.random.fold_in(key, 31)
    keys = jax.random.split(key, 3)
    noise = jnp.clip(jax.random.normal(keys[0], (NV, CH, P_SIZE), jnp.float32), -4.0, 4.0)
    coupling = jax.random.uniform(keys[1], (1, CH, 1), jnp.float32, -1.0, 1.0)
    offsets = jax.random.uniform(keys[2], (1, CH, 1), jnp.float32, -0.5, 0.5)
    return (volume_ramp(NV) * (coupling * shared + offsets + noise)).astype(jnp.bfloat16)


def block_levels(own_key, shape, shards, least, top_value):
    def one(dim, blocks):
        draws = jax.random.uniform(jax.random.fold_in(jax.random.fold_in(own_key, 6), dim), (blocks,), jnp.float32, least / len(shards), top_value / len(shards))
        return jnp.repeat(jnp.exp(draws), shape[dim] // blocks).reshape((-1,) + (1,) * (len(shape) - dim - 1))

    level = one(*shards[0])
    for cut in shards[1:]:
        level = level * one(*cut)
    return level


def gaussian(rng, extent, deviation, most, pieces=(), held_as=jnp.bfloat16):
    level = block_levels(rng, extent, pieces, -0.22, 0.18) if pieces else 1.0
    result = jax.random.normal(rng, extent, jnp.float32) * deviation * level
    return jnp.minimum(jnp.maximum(result, -most), most).astype(held_as)


def setup_inputs(seed: int = 0) -> dict:
    key_list = jax.random.split(jax.random.key(seed), 10)
    return {
        "fwd_input": draw_fwd_input(jax.random.fold_in(key_list[9], 71), 0),
        "weight_one": gaussian(key_list[1], (27, CH, CH), (27 * CH) ** -0.5, 0.078125, ((1, 64),)),
        "gain_one": jnp.clip(1.0 + 0.15 * jax.random.normal(key_list[2], (CH,), jnp.float32), 0.25, 1.75),
        "bias_one": jnp.clip(jax.random.uniform(key_list[3], (CH,), jnp.float32, -0.5, 0.5) * block_levels(key_list[3], (CH,), ((0, 64),), -0.4, 0.0), -0.5, 0.5),
        "saved_conv": draw_saved_conv(jax.random.fold_in(key_list[9], 71), 0),
        "cotangent": draw_cotangent(jax.random.fold_in(key_list[9], 71), 0),
        "saved_input": draw_saved_input(jax.random.fold_in(key_list[9], 71), 0),
        "weight_two": gaussian(key_list[7], (27, CH, CH), (27 * CH) ** -0.5, 0.078125, ((2, 64),)),
        "gain_two": jnp.clip(1.0 + 0.15 * jax.random.normal(key_list[8], (CH,), jnp.float32), 0.25, 1.75),
    }


EPSILON = 1e-05
OFFSETS = tuple(((first, second, third) for first in (-1, 0, 1) for second in (-1, 0, 1) for third in (-1, 0, 1)))

def padded_cube(volume):
    breadth = volume.shape[0]
    cube = volume.reshape(breadth, DEPTH, SIDE, SIDE)
    return jnp.pad(cube, ((0, 0), (1, 1), (1, 1), (1, 1)))

def window_at(padded, offset, direction):
    first, second, third = offset
    return padded[..., 1 + direction * first:1 + direction * first + DEPTH, 1 + direction * second:1 + direction * second + SIDE, 1 + direction * third:1 + direction * third + SIDE]

def shift_sum(stacked, direction):
    breadth = stacked.shape[1]
    cube = stacked.reshape(27, breadth, DEPTH, SIDE, SIDE)
    padded = jnp.pad(cube, ((0, 0), (0, 0), (1, 1), (1, 1), (1, 1)))
    running = jnp.zeros((breadth, DEPTH, SIDE, SIDE), jnp.float32)
    for index in range(27):
        running = running + window_at(padded[index], OFFSETS[index], direction)
    return running.reshape(breadth, DEPTH * SIDE * SIDE)

def shifted_copies(volume):
    padded = padded_cube(volume)
    breadth = volume.shape[0]
    return jnp.stack([window_at(padded, offset, 1).reshape(breadth, DEPTH * SIDE * SIDE) for offset in OFFSETS])

def reference(fwd_input, weight_one, gain_one, bias_one, saved_conv, cotangent, saved_input, weight_two, gain_two):
    counted = NV * P_SIZE
    flat_one = weight_one.reshape(27 * CH, CH)

    def forward_volume(volume):
        stacked = jnp.dot(flat_one, volume, preferred_element_type=jnp.float32).reshape(27, CH, P_SIZE)
        return shift_sum(stacked, 1)
    conv_out = lax.map(forward_volume, fwd_input)
    mean_one = lax.optimization_barrier(jnp.sum(conv_out, axis=(0, 2))) / counted
    var_one = lax.optimization_barrier(jnp.sum(conv_out * conv_out, axis=(0, 2))) / counted - mean_one * mean_one
    scale_one = gain_one * lax.rsqrt(var_one + EPSILON)
    activation = jax.nn.relu((conv_out - mean_one[None, :, None]) * scale_one[None, :, None] + bias_one[None, :, None]).astype(jnp.bfloat16)
    pre_norm = saved_conv.astype(jnp.float32)
    upstream = cotangent.astype(jnp.float32)
    mean_two = lax.optimization_barrier(jnp.sum(pre_norm, axis=(0, 2))) / counted
    var_two = lax.optimization_barrier(jnp.sum(pre_norm * pre_norm, axis=(0, 2))) / counted - mean_two * mean_two
    inverse_two = lax.rsqrt(var_two + EPSILON)
    normed = (pre_norm - mean_two[None, :, None]) * inverse_two[None, :, None]
    shift_grad = lax.optimization_barrier(jnp.sum(upstream, axis=(0, 2))) / counted
    gain_grad = lax.optimization_barrier(jnp.sum(upstream * normed, axis=(0, 2))) / counted
    conv_grad = ((gain_two * inverse_two)[None, :, None] * (upstream - shift_grad[None, :, None] - normed * gain_grad[None, :, None])).astype(jnp.bfloat16)
    flat_two = jnp.transpose(weight_two, (0, 2, 1)).reshape(27 * CH, CH)

    def backward_volume(grads):
        stacked = jnp.dot(flat_two, grads, preferred_element_type=jnp.float32).reshape(27, CH, P_SIZE)
        return shift_sum(stacked, -1).astype(jnp.bfloat16)
    input_grad = lax.map(backward_volume, conv_grad)

    def add_volume(running, paired):
        grads, acts = paired
        copies = shifted_copies(acts).astype(jnp.float32)
        term = jnp.einsum('fp,ocp->ofc', grads.astype(jnp.float32), copies, precision=lax.Precision.HIGHEST)
        return (running + term, None)
    summed = lax.scan(add_volume, jnp.zeros((27, CH, CH), jnp.float32), (conv_grad, saved_input))[0]
    weight_grad = summed / math.sqrt(counted)
    return (activation, input_grad, weight_grad, gain_grad, shift_grad)
```

```python
import math

import jax
import jax.numpy as jnp
from jax import lax
from jax.experimental import pallas as pl
from jax.experimental.pallas import tpu as pltpu
from jax.sharding import Mesh
from jax.sharding import PartitionSpec as P

PLANE = 1024
BLOCK = 1536
EDGE = 128
REACH = PLANE + EDGE
SPAN = BLOCK + 2 * REACH
CELLS = 12288
NY = 8
NZ = 8
OWN = 4
GROUP = NY * OWN
CH = 256
ROWS = 27 * GROUP
EPSILON = 1e-05
F32 = jnp.float32
BF16 = jnp.bfloat16

VMEM = pl.BlockSpec(memory_space=pltpu.VMEM)
SMEM = pl.BlockSpec(memory_space=pltpu.SMEM)
PARAMS = pltpu.CompilerParams(vmem_limit_bytes=40 * 1024 * 1024)


def iota(shape, axis):
    return lax.broadcasted_iota(jnp.int32, shape, axis)


def shift(value, amount):
    lanes = value.shape[1]
    return pltpu.roll(value, (-amount) % lanes, 1)


def nt_dot(left, right):
    return lax.dot_general(left, right, (((1,), (1,)), ((), ())), preferred_element_type=F32)


def spread(base, terms, out_ref, sign):
    def rows(group, carry):
        lane = iota((8, BLOCK), 1)
        along_x = lane & 31
        along_y = lax.shift_right_logical(lane + base, 5) & 31
        ends = {1: along_x >= 1, -1: along_x <= 30}
        sides = {1: along_y >= 1, -1: along_y <= 30}
        margin = jnp.zeros((8, EDGE), F32)
        by_plane = {}
        for a in (-1, 0, 1):
            total = None
            for b in (-1, 0, 1):
                line = None
                for c in (-1, 0, 1):
                    index = 9 * (a + 1) + 3 * (b + 1) + (c + 1)
                    term = terms[pl.ds(pl.multiple_of(index * GROUP + group * 8, 8), 8), :]
                    if c != 0:
                        term = shift(jnp.where(ends[sign * c], term, 0.0), sign * c)
                    line = term if line is None else line + term
                if b != 0:
                    line = jnp.where(sides[sign * b], line, 0.0)
                line = jnp.concatenate([margin, line, margin], axis=1)
                if b != 0:
                    line = shift(line, sign * b * 32)
                total = line if total is None else total + line
            by_plane[sign * a] = total
        low, mid, high = by_plane[1], by_plane[0], by_plane[-1]
        pieces = (
            (0, low[:, :1024]),
            (1024, low[:, 1024:] + mid[:, :768]),
            (1792, mid[:, 768:1024]),
            (2048, mid[:, 1024:] + high[:, :768]),
            (2816, high[:, 768:]),
        )
        for start, piece in pieces:
            stop = start + piece.shape[1]
            out_ref[2 * group, :, start:stop] = piece[:OWN].astype(out_ref.dtype)
            out_ref[2 * group + 1, :, start:stop] = piece[OWN:].astype(out_ref.dtype)
        return carry

    lax.fori_loop(0, GROUP // 8, rows, 0)


def forward_kernel(base_ref, weight_ref, cells_ref, out_ref, terms):
    def columns(step, carry):
        part = pl.ds(pl.multiple_of(step * 256, 256), 256)
        terms[:, part] = nt_dot(weight_ref[...], cells_ref[part, :])
        return carry

    lax.fori_loop(0, BLOCK // 256, columns, 0)
    spread(base_ref[0], terms, out_ref, 1)


def natural_rows(grads_ref, natural):
    to, of = iota((CH, CH), 0), iota((CH, CH), 1)
    same = (
        (lax.shift_right_logical(to, 5) == (lax.shift_right_logical(of, 2) & 7))
        & ((lax.shift_right_logical(to, 2) & 7) == lax.shift_right_logical(of, 5))
        & ((to & 3) == (of & 3))
    )
    select = jnp.where(same, 1.0, 0.0).astype(BF16)

    def columns(step, carry):
        part = pl.ds(pl.multiple_of(step * 256, 256), 256)
        natural[:, part] = jnp.dot(
            select, grads_ref[:, part], preferred_element_type=F32
        ).astype(BF16)
        return carry

    lax.fori_loop(0, BLOCK // 256, columns, 0)


def backward_kernel(base_ref, weight_ref, grads_ref, out_ref, natural, terms):
    natural_rows(grads_ref, natural)

    def columns(step, carry):
        part = pl.ds(pl.multiple_of(step * 256, 256), 256)
        terms[:, part] = jnp.dot(
            weight_ref[...], natural[:, part], preferred_element_type=F32
        )
        return carry

    lax.fori_loop(0, BLOCK // 256, columns, 0)
    spread(base_ref[0], terms, out_ref, -1)


def filter_kernel(base_ref, grads_ref, acts_ref, out_ref, natural, copies, product):
    natural_rows(grads_ref, natural)
    base = base_ref[0]

    def rows(group, carry):
        lane = iota((16, SPAN), 1)
        along_x = lane & 31
        along_y = lax.shift_right_logical(lane + (base + 2 * PLANE - REACH), 5) & 31
        first = pl.multiple_of(group * 16, 16)
        acts = acts_ref[pl.ds(first, 16), :].astype(F32)
        ends = {1: along_x <= 30, -1: along_x >= 1}
        sides = {1: along_y <= 30, -1: along_y >= 1}
        for b in (-1, 0, 1):
            for c in (-1, 0, 1):
                moved = acts
                if b != 0 or c != 0:
                    moved = shift(acts, 32 * b + c)
                if c != 0:
                    moved = jnp.where(ends[c], moved, 0.0)
                if b != 0:
                    moved = jnp.where(sides[b], moved, 0.0)
                moved = moved.astype(BF16)
                for a in (-1, 0, 1):
                    index = 9 * (a + 1) + 3 * (b + 1) + (c + 1)
                    start = REACH + PLANE * a
                    copies[pl.ds(index * GROUP + first, 16), :] = moved[:, start : start + BLOCK]
        return carry

    lax.fori_loop(0, GROUP // 16, rows, 0)
    copies[ROWS:, :] = jnp.zeros((1024 - ROWS, BLOCK), BF16)

    def offsets(step, carry):
        part = pl.ds(pl.multiple_of(step * 256, 256), 256)
        product[:, part] = nt_dot(natural[...], copies[part, :]).astype(BF16)
        return carry

    lax.fori_loop(0, 4, offsets, 0)

    def owners(step, carry):
        of = iota((1024, 256), 0)
        to = iota((1024, 256), 1)
        same = (
            (2 * step + lax.shift_right_logical(to, 7)) == (lax.shift_right_logical(of, 2) & 7)
        ) & ((to & 127) == (lax.shift_right_logical(of, 5) * 4 + (of & 3)))
        select = jnp.where(same, 1.0, 0.0).astype(BF16)
        placed = jnp.dot(product[...], select, preferred_element_type=F32).astype(BF16)
        for vol in range(8):
            for half in range(2):
                out_ref[vol, 2 * step + half] = placed[
                    32 * vol : 32 * vol + 32, 128 * half : 128 * half + 128
                ]
        return carry

    lax.fori_loop(0, 4, owners, 0)


def lane_sum(value):
    parts = value[:, :128]
    for start in range(128, value.shape[1], 128):
        parts = parts + value[:, start : start + 128]
    return jnp.broadcast_to(jnp.sum(parts, axis=1, keepdims=True), (value.shape[0], 128))


def prepare_kernel(saved_ref, upstream_ref, acts_ref, sums_ref, packed_ref):
    saved = saved_ref[...].astype(F32)
    upstream = upstream_ref[...].astype(F32)
    sums_ref[0] = lane_sum(saved)
    sums_ref[1] = lane_sum(saved * saved)
    sums_ref[2] = lane_sum(upstream)
    sums_ref[3] = lane_sum(upstream * saved)
    for block in range(NY):
        start = block * BLOCK - REACH
        low, high = max(start, 0), min(start + SPAN, CELLS)
        packed_ref[block, :, low - start : high - start] = acts_ref[:, low:high]
        if low > start:
            packed_ref[block, :, : low - start] = jnp.zeros((OWN, low - start), BF16)
        if high < start + SPAN:
            packed_ref[block, :, high - start :] = jnp.zeros((OWN, start + SPAN - high), BF16)


def grad_kernel(counted, saved_ref, upstream_ref, sums_ref, params_ref, packed_ref, means_ref):
    mean = sums_ref[0] / counted
    var = sums_ref[1] / counted - mean * mean
    inverse = lax.rsqrt(var + EPSILON)
    shift_grad = sums_ref[2] / counted
    gain_grad = (sums_ref[3] / counted - mean * shift_grad) * inverse
    means_ref[0] = gain_grad
    means_ref[1] = shift_grad
    scale = (params_ref[2] * inverse)[:, :1]
    mean, inverse = mean[:, :1], inverse[:, :1]
    shift_grad, gain_grad = shift_grad[:, :1], gain_grad[:, :1]
    for block in range(NY):
        part = slice(block * BLOCK, (block + 1) * BLOCK)
        normed = (saved_ref[:, part].astype(F32) - mean) * inverse
        upstream = upstream_ref[:, part].astype(F32)
        packed_ref[block] = (scale * (upstream - shift_grad - normed * gain_grad)).astype(BF16)


def joined(parts_ref, block):
    whole = parts_ref[block, :, REACH : REACH + BLOCK].astype(F32)
    pieces = [whole[:, :384], whole[:, 384:REACH], whole[:, REACH:]]
    if block > 0:
        before = parts_ref[block - 1, :, REACH + BLOCK :].astype(F32)
        pieces[0] = pieces[0] + before[:, :384]
        pieces[1] = pieces[1] + before[:, 384:]
    if block < NY - 1:
        after = parts_ref[block + 1, :, :REACH].astype(F32)
        pieces[1] = pieces[1] + after[:, : REACH - 384]
        pieces[2] = pieces[2] + after[:, REACH - 384 :]
    return jnp.concatenate(pieces, axis=1)


def join_stats_kernel(parts_ref, out_ref, sums_ref):
    total = jnp.zeros((OWN, 128), F32)
    squares = jnp.zeros((OWN, 128), F32)
    for block in range(NY):
        cells = joined(parts_ref, block)
        out_ref[:, block * BLOCK : (block + 1) * BLOCK] = cells
        total = total + lane_sum(cells)
        squares = squares + lane_sum(cells * cells)
    sums_ref[0] = total
    sums_ref[1] = squares


def join_kernel(parts_ref, out_ref):
    for block in range(NY):
        out_ref[:, block * BLOCK : (block + 1) * BLOCK] = joined(parts_ref, block).astype(BF16)


def relu_kernel(counted, conv_ref, sums_ref, params_ref, out_ref):
    mean = sums_ref[0] / counted
    var = sums_ref[1] / counted - mean * mean
    scale = (params_ref[0] * lax.rsqrt(var + EPSILON))[:, :1]
    mean, bias = mean[:, :1], params_ref[1][:, :1]
    out_ref[...] = jnp.maximum((conv_ref[...] - mean) * scale + bias, 0.0).astype(BF16)


def shaped(shape, dtype):
    return jax.ShapeDtypeStruct(shape, dtype)


def call(kernel, outs, specs, scratch=(), flops=0, moved=0):
    return pl.pallas_call(
        kernel,
        out_shape=outs,
        in_specs=specs,
        out_specs=jax.tree.map(lambda _: VMEM, outs),
        scratch_shapes=list(scratch),
        compiler_params=PARAMS,
        cost_estimate=pl.CostEstimate(flops=flops, bytes_accessed=moved, transcendentals=0),
    )


def shards(
    fwd_input,
    weight_one,
    gain_one,
    bias_one,
    saved_conv,
    cotangent,
    saved_input,
    weight_two,
    gain_two,
):
    counted = lax.axis_size("vol") * CELLS
    matmul = 2 * ROWS * CH * BLOCK
    base = (lax.axis_index("y") * BLOCK).astype(jnp.int32).reshape(1)
    params = jnp.broadcast_to(
        jnp.stack([gain_one, bias_one, gain_two])[:, :, None], (3, OWN, 128)
    )

    cells = lax.all_gather(fwd_input[0].T, "z", axis=0, tiled=True)
    both = jnp.stack([weight_one, jnp.transpose(weight_two, (0, 2, 1))])
    both = lax.all_gather(both, "y", axis=0, tiled=False)
    both = jnp.transpose(both, (1, 2, 0, 3, 4)).reshape(2, ROWS, CH)

    saved, upstream = saved_conv[0], cotangent[0]
    sums_two, acts = call(
        prepare_kernel,
        (shaped((4, OWN, 128), F32), shaped((NY, OWN, SPAN), BF16)),
        [VMEM] * 3,
        moved=600000,
    )(saved, upstream, saved_input[0])
    acts = lax.all_to_all(acts, "y", 0, 0, tiled=True).reshape(GROUP, SPAN)
    sums_two = lax.psum(sums_two, "vol")
    grads, means = call(
        lambda *refs: grad_kernel(counted, *refs),
        (shaped((NY, OWN, BLOCK), BF16), shaped((2, OWN, 128), F32)),
        [VMEM] * 4,
        moved=300000,
    )(saved, upstream, sums_two, params)
    grads = lax.all_to_all(grads, "y", 0, 0, tiled=True).reshape(GROUP, BLOCK)
    grads = lax.all_gather(grads, "z", axis=0, tiled=True)

    cells, sums_two = lax.optimization_barrier((cells, sums_two))
    conv_parts = call(
        forward_kernel,
        shaped((NY, OWN, SPAN), F32),
        [SMEM, VMEM, VMEM],
        [pltpu.VMEM((ROWS, BLOCK), F32)],
        flops=matmul,
        moved=10000000,
    )(base, both[0], cells)
    conv_parts = lax.all_to_all(conv_parts, "y", 0, 0, tiled=True)
    conv_out, sums_one = call(
        join_stats_kernel,
        (shaped((OWN, CELLS), F32), shaped((2, OWN, 128), F32)),
        [VMEM],
        moved=700000,
    )(conv_parts)
    sums_one = lax.psum(sums_one, "vol")
    sums_one, grads = lax.optimization_barrier((sums_one, grads))
    activation = call(
        lambda *refs: relu_kernel(counted, *refs),
        shaped((OWN, CELLS), BF16),
        [VMEM] * 3,
        moved=300000,
    )(conv_out, sums_one, params)

    filter_parts = call(
        filter_kernel,
        shaped((8, NY, GROUP, 128), BF16),
        [SMEM, VMEM, VMEM],
        [
            pltpu.VMEM((CH, BLOCK), BF16),
            pltpu.VMEM((1024, BLOCK), BF16),
            pltpu.VMEM((CH, 1024), BF16),
        ],
        flops=2 * matmul,
        moved=10000000,
    )(base, grads, acts)
    filter_parts = lax.all_to_all(
        filter_parts.reshape(8 * NY, GROUP, 128), ("vol", "y"), 0, 0, tiled=True
    )

    input_parts = call(
        backward_kernel,
        shaped((NY, OWN, SPAN), BF16),
        [SMEM, VMEM, VMEM],
        [pltpu.VMEM((CH, BLOCK), BF16), pltpu.VMEM((ROWS, BLOCK), F32)],
        flops=matmul,
        moved=10000000,
    )(base, both[1], grads)
    input_parts = lax.all_to_all(input_parts, "y", 0, 0, tiled=True)
    input_grad = call(join_kernel, shaped((OWN, CELLS), BF16), [VMEM], moved=350000)(input_parts)

    summed = jnp.sum(filter_parts.astype(F32), axis=0) / math.sqrt(counted)
    weight_grad = jnp.transpose(summed[:, : 27 * OWN].reshape(GROUP, 27, OWN), (1, 0, 2))
    return (activation[None], input_grad[None], weight_grad, means[0, :, 0], means[1, :, 0])


def solution(mesh):
    cut = Mesh(mesh.devices.reshape(mesh.devices.shape[0], NY, NZ), ("vol", "y", "z"))
    chan = ("y", "z")
    return jax.shard_map(
        shards,
        mesh=cut,
        in_specs=(
            P("vol", None, chan),
            P(None, chan, None),
            P(chan),
            P(chan),
            P("vol", chan, None),
            P("vol", chan, None),
            P("vol", chan, None),
            P(None, None, chan),
            P(chan),
        ),
        out_specs=(
            P("vol", chan, None),
            P("vol", chan, None),
            P(None, "vol", chan),
            P(chan),
            P(chan),
        ),
        check_vma=False,
    )
```

```python
import math

import jax
import jax.numpy as jnp
from jax import lax
from jax.experimental import pallas as pl
from jax.experimental.pallas import tpu as pltpu
from jax.sharding import Mesh
from jax.sharding import PartitionSpec as P

PLANE = 1024
BLOCK = 1536
EDGE = 128
REACH = PLANE + EDGE
SPAN = BLOCK + 2 * REACH
CELLS = 12288
NY = 8
NZ = 8
OWN = 4
GROUP = NY * OWN
CH = 256
ROWS = 27 * GROUP
EPSILON = 1e-05
F32 = jnp.float32
BF16 = jnp.bfloat16

VMEM = pl.BlockSpec(memory_space=pltpu.VMEM)
SMEM = pl.BlockSpec(memory_space=pltpu.SMEM)
PARAMS = pltpu.CompilerParams(vmem_limit_bytes=40 * 1024 * 1024)


def iota(shape, axis):
    return lax.broadcasted_iota(jnp.int32, shape, axis)


def shift(value, amount):
    lanes = value.shape[1]
    return pltpu.roll(value, (-amount) % lanes, 1)


def nt_dot(left, right):
    return lax.dot_general(left, right, (((1,), (1,)), ((), ())), preferred_element_type=F32)


def spread(base, terms, out_ref, sign):
    def rows(group, carry):
        lane = iota((8, BLOCK), 1)
        along_x = lane & 31
        along_y = lax.shift_right_logical(lane + base, 5) & 31
        ends = {1: along_x >= 1, -1: along_x <= 30}
        sides = {1: along_y >= 1, -1: along_y <= 30}
        margin = jnp.zeros((8, EDGE), F32)
        by_plane = {}
        for a in (-1, 0, 1):
            total = None
            for b in (-1, 0, 1):
                line = None
                for c in (-1, 0, 1):
                    index = 9 * (a + 1) + 3 * (b + 1) + (c + 1)
                    term = terms[pl.ds(pl.multiple_of(index * GROUP + group * 8, 8), 8), :]
                    if c != 0:
                        term = shift(jnp.where(ends[sign * c], term, 0.0), sign * c)
                    line = term if line is None else line + term
                if b != 0:
                    line = jnp.where(sides[sign * b], line, 0.0)
                line = jnp.concatenate([margin, line, margin], axis=1)
                if b != 0:
                    line = shift(line, sign * b * 32)
                total = line if total is None else total + line
            by_plane[sign * a] = total
        low, mid, high = by_plane[1], by_plane[0], by_plane[-1]
        pieces = (
            (0, low[:, :1024]),
            (1024, low[:, 1024:] + mid[:, :768]),
            (1792, mid[:, 768:1024]),
            (2048, mid[:, 1024:] + high[:, :768]),
            (2816, high[:, 768:]),
        )
        for start, piece in pieces:
            stop = start + piece.shape[1]
            out_ref[2 * group, :, start:stop] = piece[:OWN].astype(out_ref.dtype)
            out_ref[2 * group + 1, :, start:stop] = piece[OWN:].astype(out_ref.dtype)
        return carry

    lax.fori_loop(0, GROUP // 8, rows, 0)


def forward_kernel(base_ref, weight_ref, cells_ref, out_ref, terms):
    def columns(step, carry):
        part = pl.ds(pl.multiple_of(step * 256, 256), 256)
        terms[:, part] = nt_dot(weight_ref[...], cells_ref[part, :])
        return carry

    lax.fori_loop(0, BLOCK // 256, columns, 0)
    spread(base_ref[0], terms, out_ref, 1)


def backward_kernel(base_ref, weight_ref, grads_ref, out_ref, terms):
    def columns(step, carry):
        part = pl.ds(pl.multiple_of(step * 256, 256), 256)
        terms[:, part] = jnp.dot(
            weight_ref[...], grads_ref[:, part], preferred_element_type=F32
        )
        return carry

    lax.fori_loop(0, BLOCK // 256, columns, 0)
    spread(base_ref[0], terms, out_ref, -1)


def filter_kernel(base_ref, grads_ref, acts_ref, out_ref, copies, product):
    base = base_ref[0]

    def rows(group, carry):
        lane = iota((16, SPAN), 1)
        along_x = lane & 31
        along_y = lax.shift_right_logical(lane + (base + 2 * PLANE - REACH), 5) & 31
        first = pl.multiple_of(group * 16, 16)
        acts = acts_ref[pl.ds(first, 16), :].astype(F32)
        ends = {1: along_x <= 30, -1: along_x >= 1}
        sides = {1: along_y <= 30, -1: along_y >= 1}
        for b in (-1, 0, 1):
            for c in (-1, 0, 1):
                moved = acts
                if b != 0 or c != 0:
                    moved = shift(acts, 32 * b + c)
                if c != 0:
                    moved = jnp.where(ends[c], moved, 0.0)
                if b != 0:
                    moved = jnp.where(sides[b], moved, 0.0)
                moved = moved.astype(BF16)
                for a in (-1, 0, 1):
                    index = 9 * (a + 1) + 3 * (b + 1) + (c + 1)
                    start = REACH + PLANE * a
                    copies[pl.ds(index * GROUP + first, 16), :] = moved[:, start : start + BLOCK]
        return carry

    lax.fori_loop(0, GROUP // 16, rows, 0)
    copies[ROWS:, :] = jnp.zeros((1024 - ROWS, BLOCK), BF16)

    def offsets(step, carry):
        part = pl.ds(pl.multiple_of(step * 256, 256), 256)
        product[:, part] = nt_dot(grads_ref[...], copies[part, :]).astype(BF16)
        return carry

    lax.fori_loop(0, 4, offsets, 0)

    def owners(step, carry):
        of = iota((1024, 256), 0)
        to = iota((1024, 256), 1)
        same = (
            (2 * step + lax.shift_right_logical(to, 7)) == (lax.shift_right_logical(of, 2) & 7)
        ) & ((to & 127) == (lax.shift_right_logical(of, 5) * 4 + (of & 3)))
        select = jnp.where(same, 1.0, 0.0).astype(BF16)
        placed = jnp.dot(product[...], select, preferred_element_type=F32).astype(BF16)
        for vol in range(8):
            for half in range(2):
                out_ref[vol, 2 * step + half] = placed[
                    32 * vol : 32 * vol + 32, 128 * half : 128 * half + 128
                ]
        return carry

    lax.fori_loop(0, 4, owners, 0)


def lane_sum(value):
    parts = value[:, :128]
    for start in range(128, value.shape[1], 128):
        parts = parts + value[:, start : start + 128]
    return jnp.broadcast_to(jnp.sum(parts, axis=1, keepdims=True), (value.shape[0], 128))


def in_lanes(values):
    lane = iota((OWN, 128), 1)
    row = jnp.zeros((OWN, 128), F32)
    for index, value in enumerate(values):
        row = jnp.where(lane == index, value, row)
    return row


def from_lanes(sums_ref, count):
    total = sums_ref[0]
    for vol in range(1, sums_ref.shape[0]):
        total = total + sums_ref[vol]
    lane = iota((OWN, 128), 1)
    return [
        jnp.sum(jnp.where(lane == index, total, 0.0), axis=1, keepdims=True)
        for index in range(count)
    ]


def to_volumes(sums_ref, values):
    row = in_lanes(values)
    for vol in range(sums_ref.shape[0]):
        sums_ref[vol] = row


def sums_kernel(saved_hbm, upstream_hbm, sums_ref, saved_ref, upstream_ref, arrived):
    first = pltpu.make_async_copy(saved_hbm, saved_ref, arrived.at[0])
    second = pltpu.make_async_copy(upstream_hbm, upstream_ref, arrived.at[1])
    first.start()
    second.start()
    first.wait()
    second.wait()
    saved = saved_ref[...].astype(F32)
    upstream = upstream_ref[...].astype(F32)
    to_volumes(
        sums_ref,
        [
            lane_sum(saved),
            lane_sum(saved * saved),
            lane_sum(upstream),
            lane_sum(upstream * saved),
        ],
    )


def pack_kernel(acts_ref, packed_ref):
    for block in range(NY):
        start = block * BLOCK - REACH
        low, high = max(start, 0), min(start + SPAN, CELLS)
        packed_ref[block, :, low - start : high - start] = acts_ref[:, low:high]
        if low > start:
            packed_ref[block, :, : low - start] = jnp.zeros((OWN, low - start), BF16)
        if high < start + SPAN:
            packed_ref[block, :, high - start :] = jnp.zeros((OWN, start + SPAN - high), BF16)


def grad_kernel(counted, saved_ref, upstream_ref, sums_ref, params_ref, packed_ref, means_ref):
    saved_sum, square_sum, upstream_sum, product_sum = from_lanes(sums_ref, 4)
    mean = saved_sum / counted
    var = square_sum / counted - mean * mean
    inverse = lax.rsqrt(var + EPSILON)
    shift_grad = upstream_sum / counted
    gain_grad = (product_sum / counted - mean * shift_grad) * inverse
    means_ref[...] = in_lanes([gain_grad, shift_grad])
    scale = params_ref[2][:, :1] * inverse
    for block in range(NY):
        part = slice(block * BLOCK, (block + 1) * BLOCK)
        normed = (saved_ref[:, part].astype(F32) - mean) * inverse
        upstream = upstream_ref[:, part].astype(F32)
        grads = (scale * (upstream - shift_grad - normed * gain_grad)).astype(BF16)
        for to in range(NZ):
            packed_ref[block * NZ + to] = grads


def joined(parts_ref, block):
    whole = parts_ref[block, :, REACH : REACH + BLOCK].astype(F32)
    pieces = [whole[:, :384], whole[:, 384:REACH], whole[:, REACH:]]
    if block > 0:
        before = parts_ref[block - 1, :, REACH + BLOCK :].astype(F32)
        pieces[0] = pieces[0] + before[:, :384]
        pieces[1] = pieces[1] + before[:, 384:]
    if block < NY - 1:
        after = parts_ref[block + 1, :, :REACH].astype(F32)
        pieces[1] = pieces[1] + after[:, : REACH - 384]
        pieces[2] = pieces[2] + after[:, REACH - 384 :]
    return jnp.concatenate(pieces, axis=1)


def join_stats_kernel(parts_ref, out_ref, sums_ref):
    total = jnp.zeros((OWN, 128), F32)
    squares = jnp.zeros((OWN, 128), F32)
    for block in range(NY):
        cells = joined(parts_ref, block)
        out_ref[:, block * BLOCK : (block + 1) * BLOCK] = cells
        total = total + lane_sum(cells)
        squares = squares + lane_sum(cells * cells)
    to_volumes(sums_ref, [total, squares])


def join_kernel(parts_ref, out_ref):
    for block in range(NY):
        out_ref[:, block * BLOCK : (block + 1) * BLOCK] = joined(parts_ref, block).astype(BF16)


def relu_kernel(counted, conv_ref, sums_ref, params_ref, out_ref):
    first_sum, square_sum = from_lanes(sums_ref, 2)
    mean = first_sum / counted
    var = square_sum / counted - mean * mean
    scale = params_ref[0][:, :1] * lax.rsqrt(var + EPSILON)
    bias = params_ref[1][:, :1]
    out_ref[...] = jnp.maximum((conv_ref[...] - mean) * scale + bias, 0.0).astype(BF16)


def shaped(shape, dtype):
    return jax.ShapeDtypeStruct(shape, dtype)


def call(kernel, outs, specs, scratch=()):
    return pl.pallas_call(
        kernel,
        out_shape=outs,
        in_specs=specs,
        out_specs=jax.tree.map(lambda _: VMEM, outs),
        scratch_shapes=list(scratch),
        compiler_params=PARAMS,
        cost_estimate=pl.CostEstimate(flops=1000, bytes_accessed=1000, transcendentals=0),
    )


def exchange(value, axes):
    return lax.all_to_all(value, axes, 0, 0, tiled=True)


def to_all(value, axis):
    return exchange(jnp.broadcast_to(value[None], (lax.axis_size(axis),) + value.shape), axis)


def shards(
    fwd_input,
    weight_one,
    gain_one,
    bias_one,
    saved_conv,
    cotangent,
    saved_input,
    weight_two,
    gain_two,
):
    volumes = lax.axis_size("vol")
    counted = volumes * CELLS
    base = (lax.axis_index("y") * BLOCK).astype(jnp.int32).reshape(1)
    params = jnp.broadcast_to(
        jnp.stack([gain_one, bias_one, gain_two])[:, :, None], (3, OWN, 128)
    )
    saved, upstream = saved_conv[0], cotangent[0]

    sums_two = call(
        sums_kernel,
        shaped((volumes, OWN, 128), F32),
        [pl.BlockSpec(memory_space=pl.ANY)] * 2,
        [
            pltpu.VMEM((OWN, CELLS), BF16),
            pltpu.VMEM((OWN, CELLS), BF16),
            pltpu.SemaphoreType.DMA((2,)),
        ],
    )(saved, upstream)
    weight_one, sums_two = lax.optimization_barrier((weight_one, sums_two))
    sums_two = exchange(sums_two, "vol")

    cells = to_all(fwd_input[0].T, "z").reshape(BLOCK, CH)
    rows = jnp.concatenate(
        [jnp.transpose(weight_one, (1, 0, 2)), jnp.transpose(weight_two, (2, 0, 1))]
    )
    row = lax.dynamic_index_in_dim(rows, lax.axis_index("vol"), 0, keepdims=False)
    rows = to_all(to_all(row, "y"), "vol")
    weights = [
        jnp.transpose(rows[first : first + OWN], (2, 1, 0, 3)).reshape(ROWS, CH)
        for first in (0, OWN)
    ]
    acts = call(pack_kernel, shaped((NY, OWN, SPAN), BF16), [VMEM])(saved_input[0])
    acts = exchange(acts, "y").reshape(GROUP, SPAN)

    packed, means = call(
        lambda *refs: grad_kernel(counted, *refs),
        (shaped((NY * NZ, OWN, BLOCK), BF16), shaped((OWN, 128), F32)),
        [VMEM] * 4,
    )(saved, upstream, sums_two, params)
    grads = exchange(packed, ("y", "z")).reshape(CH, BLOCK)

    cells, means = lax.optimization_barrier((cells, means))
    conv_parts = call(
        forward_kernel,
        shaped((NY, OWN, SPAN), F32),
        [SMEM, VMEM, VMEM],
        [pltpu.VMEM((ROWS, BLOCK), F32)],
    )(base, weights[0], cells)
    grads, conv_parts = lax.optimization_barrier((grads, conv_parts))
    conv_parts = exchange(conv_parts, "y")
    filter_parts = call(
        filter_kernel,
        shaped((8, NY, GROUP, 128), BF16),
        [SMEM, VMEM, VMEM],
        [pltpu.VMEM((1024, BLOCK), BF16), pltpu.VMEM((CH, 1024), BF16)],
    )(base, grads, acts)
    weight, filter_parts = lax.optimization_barrier((weights[1], filter_parts))
    filter_parts = exchange(filter_parts.reshape(8 * NY, GROUP, 128), ("vol", "y"))
    input_parts = call(
        backward_kernel,
        shaped((NY, OWN, SPAN), BF16),
        [SMEM, VMEM, VMEM],
        [pltpu.VMEM((ROWS, BLOCK), F32)],
    )(base, weight, grads)
    conv_parts, input_parts = lax.optimization_barrier((conv_parts, input_parts))
    input_parts = exchange(input_parts, "y")

    conv_out, sums_one = call(
        join_stats_kernel,
        (shaped((OWN, CELLS), F32), shaped((volumes, OWN, 128), F32)),
        [VMEM],
    )(conv_parts)
    sums_one = exchange(sums_one, "vol")
    activation = call(
        lambda *refs: relu_kernel(counted, *refs), shaped((OWN, CELLS), BF16), [VMEM] * 3
    )(conv_out, sums_one, params)
    input_grad = call(join_kernel, shaped((OWN, CELLS), BF16), [VMEM])(input_parts)

    summed = jnp.sum(filter_parts.astype(F32), axis=0) / math.sqrt(counted)
    weight_grad = jnp.transpose(summed[:, : 27 * OWN].reshape(GROUP, 27, OWN), (1, 0, 2))
    return (activation[None], input_grad[None], weight_grad, means[:, 0], means[:, 1])


def solution(mesh):
    cut = Mesh(mesh.devices.reshape(mesh.devices.shape[0], NY, NZ), ("vol", "y", "z"))
    chan = ("y", "z")
    return jax.shard_map(
        shards,
        mesh=cut,
        in_specs=(
            P("vol", None, chan),
            P(None, chan, None),
            P(chan),
            P(chan),
            P("vol", chan, None),
            P("vol", chan, None),
            P("vol", chan, None),
            P(None, None, chan),
            P(chan),
        ),
        out_specs=(
            P("vol", chan, None),
            P("vol", chan, None),
            P(None, "vol", chan),
            P(chan),
            P(chan),
        ),
        check_vma=False,
    )
```

```python
import math

import jax
import jax.numpy as jnp
from jax import lax
from jax.experimental import pallas as pl
from jax.experimental.pallas import tpu as pltpu
from jax.sharding import Mesh
from jax.sharding import PartitionSpec as P

PLANE = 1024
BLOCK = 1536
EDGE = 128
REACH = PLANE + EDGE
SPAN = BLOCK + 2 * REACH
CELLS = 12288
NY = 8
NZ = 8
OWN = 4
GROUP = NY * OWN
CH = 256
ROWS = 27 * GROUP
RING = (0, 1, -1, 2, -2, 3, -3, 4)
EPSILON = 1e-05
F32 = jnp.float32
BF16 = jnp.bfloat16

VMEM = pl.BlockSpec(memory_space=pltpu.VMEM)
SMEM = pl.BlockSpec(memory_space=pltpu.SMEM)
PARAMS = pltpu.CompilerParams(vmem_limit_bytes=40 * 1024 * 1024)


def iota(shape, axis):
    return lax.broadcasted_iota(jnp.int32, shape, axis)


def shift(value, amount):
    lanes = value.shape[1]
    return pltpu.roll(value, (-amount) % lanes, 1)


def nt_dot(left, right):
    return lax.dot_general(left, right, (((1,), (1,)), ((), ())), preferred_element_type=F32)


def spread(base, terms, held, out_refs, sign):
    def rows(group, carry):
        lane = iota((8, BLOCK), 1)
        along_x = lane & 31
        along_y = lax.shift_right_logical(lane + base, 5) & 31
        ends = {1: along_x >= 1, -1: along_x <= 30}
        sides = {1: along_y >= 1, -1: along_y <= 30}
        margin = jnp.zeros((8, EDGE), F32)
        by_plane = {}
        for a in (-1, 0, 1):
            total = None
            for b in (-1, 0, 1):
                line = None
                for c in (-1, 0, 1):
                    index = 9 * (a + 1) + 3 * (b + 1) + (c + 1)
                    term = terms[pl.ds(pl.multiple_of(index * GROUP + group * 8, 8), 8), :]
                    if c != 0:
                        term = shift(jnp.where(ends[sign * c], term, 0.0), sign * c)
                    line = term if line is None else line + term
                if b != 0:
                    line = jnp.where(sides[sign * b], line, 0.0)
                line = jnp.concatenate([margin, line, margin], axis=1)
                if b != 0:
                    line = shift(line, sign * b * 32)
                total = line if total is None else total + line
            by_plane[sign * a] = total
        low, mid, high = by_plane[1], by_plane[0], by_plane[-1]
        pieces = (
            (0, low[:, :1024]),
            (1024, low[:, 1024:] + mid[:, :768]),
            (1792, mid[:, 768:1024]),
            (2048, mid[:, 1024:] + high[:, :768]),
            (2816, high[:, 768:]),
        )
        for start, piece in pieces:
            stop = start + piece.shape[1]
            held[2 * group, :, start:stop] = piece[:OWN]
            held[2 * group + 1, :, start:stop] = piece[OWN:]
        return carry

    lax.fori_loop(0, GROUP // 8, rows, 0)
    for hop, out_ref in enumerate(out_refs):
        out_ref[...] = held[hop].astype(out_ref.dtype)


def forward_kernel(place_ref, weight_ref, *refs):
    parts, out_refs = refs[:NZ], refs[NZ : NZ + NY]
    cells, terms, held = refs[NZ + NY :]
    for hop, part in zip(RING, parts):
        source = (place_ref[1] - hop) & (NZ - 1)
        rows = BLOCK // NZ
        cells[pl.ds(pl.multiple_of(source * rows, rows), rows), :] = part[...]

    def columns(step, carry):
        part = pl.ds(pl.multiple_of(step * 256, 256), 256)
        terms[:, part] = nt_dot(weight_ref[...], cells[part, :])
        return carry

    lax.fori_loop(0, BLOCK // 256, columns, 0)
    spread(place_ref[0] * BLOCK, terms, held, out_refs, 1)


def backward_kernel(place_ref, weight_ref, grads_ref, *refs):
    out_refs, (terms, held) = refs[:NY], refs[NY:]

    def columns(step, carry):
        part = pl.ds(pl.multiple_of(step * 256, 256), 256)
        terms[:, part] = jnp.dot(
            weight_ref[...], grads_ref[:, part], preferred_element_type=F32
        )
        return carry

    lax.fori_loop(0, BLOCK // 256, columns, 0)
    spread(place_ref[0] * BLOCK, terms, held, out_refs, -1)


def filter_kernel(place_ref, grads_ref, *refs):
    parts, (out_ref, acts_all, copies, product) = refs[:NY], refs[NY:]
    base = place_ref[0] * BLOCK
    for hop, part in enumerate(parts):
        acts_all[OWN * hop : OWN * hop + OWN, :] = part[...].astype(F32)

    def rows(group, carry):
        lane = iota((16, SPAN), 1)
        along_x = lane & 31
        along_y = lax.shift_right_logical(lane + (base + 2 * PLANE - REACH), 5) & 31
        first = pl.multiple_of(group * 16, 16)
        acts = acts_all[pl.ds(first, 16), :]
        ends = {1: along_x <= 30, -1: along_x >= 1}
        sides = {1: along_y <= 30, -1: along_y >= 1}
        for b in (-1, 0, 1):
            for c in (-1, 0, 1):
                moved = acts
                if b != 0 or c != 0:
                    moved = shift(acts, 32 * b + c)
                if c != 0:
                    moved = jnp.where(ends[c], moved, 0.0)
                if b != 0:
                    moved = jnp.where(sides[b], moved, 0.0)
                moved = moved.astype(BF16)
                for a in (-1, 0, 1):
                    index = 9 * (a + 1) + 3 * (b + 1) + (c + 1)
                    start = REACH + PLANE * a
                    copies[pl.ds(index * GROUP + first, 16), :] = moved[:, start : start + BLOCK]
        return carry

    lax.fori_loop(0, GROUP // 16, rows, 0)
    copies[ROWS:, :] = jnp.zeros((1024 - ROWS, BLOCK), BF16)

    def offsets(step, carry):
        part = pl.ds(pl.multiple_of(step * 256, 256), 256)
        product[:, part] = nt_dot(grads_ref[...], copies[part, :]).astype(BF16)
        return carry

    lax.fori_loop(0, 4, offsets, 0)

    def owners(step, carry):
        of = iota((1024, 256), 0)
        to = iota((1024, 256), 1)
        same = (
            (2 * step + lax.shift_right_logical(to, 7)) == (lax.shift_right_logical(of, 2) & 7)
        ) & ((to & 127) == (lax.shift_right_logical(of, 5) * 4 + (of & 3)))
        select = jnp.where(same, 1.0, 0.0).astype(BF16)
        placed = jnp.dot(product[...], select, preferred_element_type=F32).astype(BF16)
        for vol in range(8):
            for half in range(2):
                owner = (place_ref[0] - (2 * step + half)) & (NY - 1)
                out_ref[vol, owner] = placed[
                    32 * vol : 32 * vol + 32, 128 * half : 128 * half + 128
                ]
        return carry

    lax.fori_loop(0, 4, owners, 0)


def lane_sum(value):
    parts = value[:, :128]
    for start in range(128, value.shape[1], 128):
        parts = parts + value[:, start : start + 128]
    return jnp.broadcast_to(jnp.sum(parts, axis=1, keepdims=True), (value.shape[0], 128))


def in_lanes(values):
    lane = iota((OWN, 128), 1)
    row = jnp.zeros((OWN, 128), F32)
    for index, value in enumerate(values):
        row = jnp.where(lane == index, value, row)
    return row


def from_lanes(sums, count):
    total = sums[0][...]
    for row in sums[1:]:
        total = total + row[...]
    lane = iota((OWN, 128), 1)
    return [
        jnp.sum(jnp.where(lane == index, total, 0.0), axis=1, keepdims=True)
        for index in range(count)
    ]


def to_volumes(sums_ref, values):
    row = in_lanes(values)
    for vol in range(sums_ref.shape[0]):
        sums_ref[vol] = row


def sums_kernel(saved_hbm, upstream_hbm, sums_ref, saved_ref, upstream_ref, arrived):
    first = pltpu.make_async_copy(saved_hbm, saved_ref, arrived.at[0])
    second = pltpu.make_async_copy(upstream_hbm, upstream_ref, arrived.at[1])
    first.start()
    second.start()
    first.wait()
    second.wait()
    saved = saved_ref[...].astype(F32)
    upstream = upstream_ref[...].astype(F32)
    to_volumes(
        sums_ref,
        [
            lane_sum(saved),
            lane_sum(saved * saved),
            lane_sum(upstream),
            lane_sum(upstream * saved),
        ],
    )


def pack_kernel(place_ref, acts_ref, *refs):
    out_refs, (padded,) = refs[:NY], refs[NY:]
    padded[:, :REACH] = jnp.zeros((OWN, REACH), F32)
    padded[:, REACH : REACH + CELLS] = acts_ref[...].astype(F32)
    padded[:, REACH + CELLS :] = jnp.zeros((OWN, REACH), F32)
    for hop, out_ref in enumerate(out_refs):
        block = (place_ref[0] + hop) & (NY - 1)
        part = padded[:, pl.ds(pl.multiple_of(block * BLOCK, BLOCK), SPAN)]
        out_ref[...] = part.astype(BF16)


def arrange_kernel(place_ref, *refs):
    parts, (first_ref, second_ref, held) = refs[:8], refs[8:]
    for hop, part in enumerate(parts):
        held[(place_ref[2] - hop) & 7] = part[...]
    to, of = iota((ROWS, 1024), 0), iota((ROWS, 1024), 1)
    same = (
        (lax.shift_right_logical(to, 5) == (of & 31))
        & ((lax.shift_right_logical(to, 2) & 7) == (lax.shift_right_logical(of, 5) & 7))
        & ((to & 3) == lax.shift_right_logical(of, 8))
    )
    select = jnp.where(same, 1.0, 0.0).astype(BF16)
    for start, out_ref in ((0, first_ref), (OWN, second_ref)):
        rows = held[start : start + OWN].reshape(1024, CH)
        out_ref[...] = jnp.dot(select, rows, preferred_element_type=F32).astype(BF16)


def grad_kernel(counted, saved_ref, upstream_ref, sums_ref, params_ref, packed_ref, means_ref):
    saved_sum, square_sum, upstream_sum, product_sum = from_lanes([sums_ref.at[vol] for vol in range(sums_ref.shape[0])], 4)
    mean = saved_sum / counted
    var = square_sum / counted - mean * mean
    inverse = lax.rsqrt(var + EPSILON)
    shift_grad = upstream_sum / counted
    gain_grad = (product_sum / counted - mean * shift_grad) * inverse
    means_ref[...] = in_lanes([gain_grad, shift_grad])
    scale = params_ref[2][:, :1] * inverse
    for block in range(NY):
        part = slice(block * BLOCK, (block + 1) * BLOCK)
        normed = (saved_ref[:, part].astype(F32) - mean) * inverse
        upstream = upstream_ref[:, part].astype(F32)
        grads = (scale * (upstream - shift_grad - normed * gain_grad)).astype(BF16)
        for to in range(NZ):
            packed_ref[block * NZ + to] = grads


def joined(parts_ref, block):
    whole = parts_ref[block, :, REACH : REACH + BLOCK].astype(F32)
    pieces = [whole[:, :384], whole[:, 384:REACH], whole[:, REACH:]]
    if block > 0:
        before = parts_ref[block - 1, :, REACH + BLOCK :].astype(F32)
        pieces[0] = pieces[0] + before[:, :384]
        pieces[1] = pieces[1] + before[:, 384:]
    if block < NY - 1:
        after = parts_ref[block + 1, :, :REACH].astype(F32)
        pieces[1] = pieces[1] + after[:, : REACH - 384]
        pieces[2] = pieces[2] + after[:, REACH - 384 :]
    return jnp.concatenate(pieces, axis=1)


def place_blocks(place_ref, parts, held):
    for hop, part in enumerate(parts):
        held[(place_ref[0] + hop) & (NY - 1)] = part[...].astype(F32)


def join_stats_kernel(place_ref, *refs):
    parts, (out_ref, sums_ref, parts_ref) = refs[:NY], refs[NY:]
    place_blocks(place_ref, parts, parts_ref)
    total = jnp.zeros((OWN, 128), F32)
    squares = jnp.zeros((OWN, 128), F32)
    for block in range(NY):
        cells = joined(parts_ref, block)
        out_ref[:, block * BLOCK : (block + 1) * BLOCK] = cells
        total = total + lane_sum(cells)
        squares = squares + lane_sum(cells * cells)
    sums_ref[...] = in_lanes([total, squares])


def join_kernel(place_ref, *refs):
    parts, (out_ref, parts_ref) = refs[:NY], refs[NY:]
    place_blocks(place_ref, parts, parts_ref)
    for block in range(NY):
        out_ref[:, block * BLOCK : (block + 1) * BLOCK] = joined(parts_ref, block).astype(BF16)


def relu_kernel(counted, conv_ref, params_ref, *refs):
    sums, out_ref = refs[:-1], refs[-1]
    first_sum, square_sum = from_lanes(sums, 2)
    mean = first_sum / counted
    var = square_sum / counted - mean * mean
    scale = params_ref[0][:, :1] * lax.rsqrt(var + EPSILON)
    bias = params_ref[1][:, :1]
    out_ref[...] = jnp.maximum((conv_ref[...] - mean) * scale + bias, 0.0).astype(BF16)


def shaped(shape, dtype):
    return jax.ShapeDtypeStruct(shape, dtype)


def call(kernel, outs, specs, scratch=()):
    return pl.pallas_call(
        kernel,
        out_shape=outs,
        in_specs=specs,
        out_specs=jax.tree.map(lambda _: VMEM, outs),
        scratch_shapes=list(scratch),
        compiler_params=PARAMS,
        cost_estimate=pl.CostEstimate(flops=1000, bytes_accessed=1000, transcendentals=0),
    )


def exchange(value, axes):
    return lax.all_to_all(value, axes, 0, 0, tiled=True)


def hop_to(value, axis, hop):
    size = lax.axis_size(axis)
    return lax.ppermute(value, axis, [(at, (at + hop) % size) for at in range(size)])


def by_hop(values, axis, sign=1):
    return [
        value if hop == 0 else hop_to(value, axis, sign * hop) for hop, value in enumerate(values)
    ]


def round_ring(value, axis):
    held = {0: value}
    for hop in range(1, NZ // 2 + 1):
        held[hop] = hop_to(held[hop - 1], axis, 1)
        if hop < NZ // 2:
            held[-hop] = hop_to(held[1 - hop], axis, -1)
    return [held[hop] for hop in RING]


def shards(
    fwd_input,
    weight_one,
    gain_one,
    bias_one,
    saved_conv,
    cotangent,
    saved_input,
    weight_two,
    gain_two,
):
    volumes = lax.axis_size("vol")
    counted = volumes * CELLS
    place = jnp.stack([lax.axis_index(name) for name in ("y", "z", "vol")]).astype(jnp.int32)
    params = jnp.broadcast_to(
        jnp.stack([gain_one, bias_one, gain_two])[:, :, None], (3, OWN, 128)
    )
    saved, upstream = saved_conv[0], cotangent[0]

    sums_two = call(
        sums_kernel,
        shaped((volumes, OWN, 128), F32),
        [pl.BlockSpec(memory_space=pl.ANY)] * 2,
        [
            pltpu.VMEM((OWN, CELLS), BF16),
            pltpu.VMEM((OWN, CELLS), BF16),
            pltpu.SemaphoreType.DMA((2,)),
        ],
    )(saved, upstream)
    weight_one, weight_two, fwd_input, sums_two = lax.optimization_barrier(
        (weight_one, weight_two, fwd_input, sums_two)
    )
    sums_two = exchange(sums_two, "vol")

    cells = round_ring(fwd_input[0].T, "z")
    rows = jnp.concatenate(
        [jnp.transpose(weight_one, (1, 0, 2)), jnp.transpose(weight_two, (2, 0, 1))]
    )
    row = lax.dynamic_index_in_dim(rows, lax.axis_index("vol"), 0, keepdims=False)
    row = jnp.pad(row, ((0, 5), (0, 0)))
    rows = jnp.stack(by_hop([row] * NY, "y"))
    weights = call(
        arrange_kernel,
        (shaped((ROWS, CH), BF16), shaped((ROWS, CH), BF16)),
        [SMEM] + [VMEM] * 8,
        [pltpu.VMEM((8, NY, 32, CH), BF16)],
    )(place, *by_hop([rows] * 8, "vol"))
    acts = call(
        pack_kernel,
        [shaped((OWN, SPAN), BF16)] * NY,
        [SMEM, VMEM],
        [pltpu.VMEM((OWN, CELLS + 2 * REACH), F32)],
    )(place, saved_input[0])
    acts = by_hop(acts, "y")

    packed, means = call(
        lambda *refs: grad_kernel(counted, *refs),
        (shaped((NY * NZ, OWN, BLOCK), BF16), shaped((OWN, 128), F32)),
        [VMEM] * 4,
    )(saved, upstream, sums_two, params)
    grads = exchange(packed, ("y", "z")).reshape(CH, BLOCK)

    cells, means = lax.optimization_barrier((cells, means))
    conv_parts = call(
        forward_kernel,
        [shaped((OWN, SPAN), F32)] * NY,
        [SMEM] + [VMEM] * (1 + NZ),
        [
            pltpu.VMEM((BLOCK, CH), BF16),
            pltpu.VMEM((ROWS, BLOCK), F32),
            pltpu.VMEM((NY, OWN, SPAN), F32),
        ],
    )(place, weights[0], *cells)
    grads, conv_parts = lax.optimization_barrier((grads, conv_parts))
    conv_parts = by_hop(conv_parts, "y", -1)
    filter_parts = call(
        filter_kernel,
        shaped((8, NY, GROUP, 128), BF16),
        [SMEM] + [VMEM] * (1 + NY),
        [
            pltpu.VMEM((GROUP, SPAN), F32),
            pltpu.VMEM((1024, BLOCK), BF16),
            pltpu.VMEM((CH, 1024), BF16),
        ],
    )(place, grads, *acts)
    weight, filter_parts = lax.optimization_barrier((weights[1], filter_parts))
    filter_parts = exchange(filter_parts.reshape(8 * NY, GROUP, 128), ("vol", "y"))
    input_parts = call(
        backward_kernel,
        [shaped((OWN, SPAN), BF16)] * NY,
        [SMEM, VMEM, VMEM],
        [pltpu.VMEM((ROWS, BLOCK), F32), pltpu.VMEM((NY, OWN, SPAN), F32)],
    )(place, weight, grads)
    conv_parts, input_parts = lax.optimization_barrier((conv_parts, input_parts))
    input_parts = by_hop(input_parts, "y", -1)

    conv_out, sums_one = call(
        join_stats_kernel,
        (shaped((OWN, CELLS), F32), shaped((OWN, 128), F32)),
        [SMEM] + [VMEM] * NY,
        [pltpu.VMEM((NY, OWN, SPAN), F32)],
    )(place, *conv_parts)
    sums_one = by_hop([sums_one] * 8, "vol")
    activation = call(
        lambda *refs: relu_kernel(counted, *refs), shaped((OWN, CELLS), BF16), [VMEM] * 10
    )(conv_out, params, *sums_one)
    input_grad = call(
        join_kernel,
        shaped((OWN, CELLS), BF16),
        [SMEM] + [VMEM] * NY,
        [pltpu.VMEM((NY, OWN, SPAN), F32)],
    )(place, *input_parts)

    summed = jnp.sum(filter_parts.astype(F32), axis=0) / math.sqrt(counted)
    weight_grad = jnp.transpose(summed[:, : 27 * OWN].reshape(GROUP, 27, OWN), (1, 0, 2))
    return (activation[None], input_grad[None], weight_grad, means[:, 0], means[:, 1])


def solution(mesh):
    cut = Mesh(mesh.devices.reshape(mesh.devices.shape[0], NY, NZ), ("vol", "y", "z"))
    chan = ("y", "z")
    return jax.shard_map(
        shards,
        mesh=cut,
        in_specs=(
            P("vol", None, chan),
            P(None, chan, None),
            P(chan),
            P(chan),
            P("vol", chan, None),
            P("vol", chan, None),
            P("vol", chan, None),
            P(None, None, chan),
            P(chan),
        ),
        out_specs=(
            P("vol", chan, None),
            P("vol", chan, None),
            P(None, "vol", chan),
            P(chan),
            P(chan),
        ),
        check_vma=False,
    )
```

```python
import math

import jax
import jax.numpy as jnp
from jax import lax
from jax.experimental import pallas as pl
from jax.experimental.pallas import tpu as pltpu
from jax.sharding import Mesh
from jax.sharding import PartitionSpec as P

PLANE = 1024
BLOCK = 1536
EDGE = 128
REACH = PLANE + EDGE
SPAN = BLOCK + 2 * REACH
CELLS = 12288
HALF = 6144
NY = 8
NZ = 8
OWN = 4
GROUP = NY * OWN
CH = 256
ROWS = 27 * GROUP
EPSILON = 1e-05
F32 = jnp.float32
BF16 = jnp.bfloat16

VMEM = pl.BlockSpec(memory_space=pltpu.VMEM)
SMEM = pl.BlockSpec(memory_space=pltpu.SMEM)
PARAMS = pltpu.CompilerParams(vmem_limit_bytes=40 * 1024 * 1024)


def iota(shape, axis):
    return lax.broadcasted_iota(jnp.int32, shape, axis)


def shift(value, amount):
    lanes = value.shape[1]
    return pltpu.roll(value, (-amount) % lanes, 1)


def nt_dot(left, right):
    return lax.dot_general(left, right, (((1,), (1,)), ((), ())), preferred_element_type=F32)


def spread(base, terms, out_ref, sign):
    def rows(group, carry):
        lane = iota((8, BLOCK), 1)
        along_x = lane & 31
        along_y = lax.shift_right_logical(lane + base, 5) & 31
        ends = {1: along_x >= 1, -1: along_x <= 30}
        sides = {1: along_y >= 1, -1: along_y <= 30}
        margin = jnp.zeros((8, EDGE), F32)
        by_plane = {}
        for a in (-1, 0, 1):
            total = None
            for b in (-1, 0, 1):
                line = None
                for c in (-1, 0, 1):
                    index = 9 * (a + 1) + 3 * (b + 1) + (c + 1)
                    term = terms[pl.ds(pl.multiple_of(index * GROUP + group * 8, 8), 8), :]
                    if c != 0:
                        term = shift(jnp.where(ends[sign * c], term, 0.0), sign * c)
                    line = term if line is None else line + term
                if b != 0:
                    line = jnp.where(sides[sign * b], line, 0.0)
                line = jnp.concatenate([margin, line, margin], axis=1)
                if b != 0:
                    line = shift(line, sign * b * 32)
                total = line if total is None else total + line
            by_plane[sign * a] = total
        low, mid, high = by_plane[1], by_plane[0], by_plane[-1]
        pieces = (
            (0, low[:, :1024]),
            (1024, low[:, 1024:] + mid[:, :768]),
            (1792, mid[:, 768:1024]),
            (2048, mid[:, 1024:] + high[:, :768]),
            (2816, high[:, 768:]),
        )
        for start, piece in pieces:
            stop = start + piece.shape[1]
            out_ref[2 * group, :, start:stop] = piece[:OWN].astype(out_ref.dtype)
            out_ref[2 * group + 1, :, start:stop] = piece[OWN:].astype(out_ref.dtype)
        return carry

    lax.fori_loop(0, GROUP // 8, rows, 0)


def forward_kernel(weight_ref, cells_ref, own_ref, other_ref, terms, held):
    def columns(step, carry):
        part = pl.ds(pl.multiple_of(step * 256, 256), 256)
        terms[:, part] = nt_dot(weight_ref[...], cells_ref[part, :])
        return carry

    lax.fori_loop(0, HALF // 256, columns, 0)
    held[...] = jnp.zeros_like(held)

    def plane(at, carry):
        lane = iota((8, PLANE), 1)
        along_x, along_y = lane & 31, lax.shift_right_logical(lane, 5)
        ends = {1: along_x >= 1, -1: along_x <= 30}
        sides = {1: along_y >= 1, -1: along_y <= 30}
        part = pl.ds(pl.multiple_of(at * PLANE, PLANE), PLANE)
        for a in (-1, 0, 1):
            total = None
            for b in (-1, 0, 1):
                line = None
                for c in (-1, 0, 1):
                    index = 9 * (a + 1) + 3 * (b + 1) + (c + 1)
                    term = terms[8 * index : 8 * index + 8, part]
                    if c != 0:
                        term = shift(jnp.where(ends[c], term, 0.0), c)
                    line = term if line is None else line + term
                if b != 0:
                    line = shift(jnp.where(sides[b], line, 0.0), 32 * b)
                total = line if total is None else total + line
            goal = pl.ds(pl.multiple_of((at + 1 - a) * PLANE, PLANE), PLANE)
            held[:, goal] += total
        return carry

    lax.fori_loop(0, HALF // PLANE, plane, 0)
    own_ref[...] = held[:OWN]
    other_ref[...] = held[OWN:]


def backward_kernel(base_ref, weight_ref, grads_ref, out_ref, terms):
    def columns(step, carry):
        part = pl.ds(pl.multiple_of(step * 256, 256), 256)
        terms[:, part] = jnp.dot(
            weight_ref[...], grads_ref[:, part], preferred_element_type=F32
        )
        return carry

    lax.fori_loop(0, BLOCK // 256, columns, 0)
    spread(base_ref[0], terms, out_ref, -1)


def filter_kernel(base_ref, grads_ref, acts_ref, out_ref, copies, product):
    base = base_ref[0]

    def rows(group, carry):
        lane = iota((16, SPAN), 1)
        along_x = lane & 31
        along_y = lax.shift_right_logical(lane + (base + 2 * PLANE - REACH), 5) & 31
        first = pl.multiple_of(group * 16, 16)
        acts = acts_ref[pl.ds(first, 16), :].astype(F32)
        ends = {1: along_x <= 30, -1: along_x >= 1}
        sides = {1: along_y <= 30, -1: along_y >= 1}
        for b in (-1, 0, 1):
            for c in (-1, 0, 1):
                moved = acts
                if b != 0 or c != 0:
                    moved = shift(acts, 32 * b + c)
                if c != 0:
                    moved = jnp.where(ends[c], moved, 0.0)
                if b != 0:
                    moved = jnp.where(sides[b], moved, 0.0)
                moved = moved.astype(BF16)
                for a in (-1, 0, 1):
                    index = 9 * (a + 1) + 3 * (b + 1) + (c + 1)
                    start = REACH + PLANE * a
                    copies[pl.ds(index * GROUP + first, 16), :] = moved[:, start : start + BLOCK]
        return carry

    lax.fori_loop(0, GROUP // 16, rows, 0)
    copies[ROWS:, :] = jnp.zeros((1024 - ROWS, BLOCK), BF16)

    def offsets(step, carry):
        part = pl.ds(pl.multiple_of(step * 256, 256), 256)
        product[:, part] = nt_dot(grads_ref[...], copies[part, :]).astype(BF16)
        return carry

    lax.fori_loop(0, 4, offsets, 0)

    def owners(step, carry):
        of = iota((1024, 256), 0)
        to = iota((1024, 256), 1)
        same = (
            (2 * step + lax.shift_right_logical(to, 7)) == (lax.shift_right_logical(of, 2) & 7)
        ) & ((to & 127) == (lax.shift_right_logical(of, 5) * 4 + (of & 3)))
        select = jnp.where(same, 1.0, 0.0).astype(BF16)
        placed = jnp.dot(product[...], select, preferred_element_type=F32).astype(BF16)
        for vol in range(8):
            for half in range(2):
                out_ref[vol, 2 * step + half] = placed[
                    32 * vol : 32 * vol + 32, 128 * half : 128 * half + 128
                ]
        return carry

    lax.fori_loop(0, 4, owners, 0)


def lane_sum(value):
    parts = value[:, :128]
    for start in range(128, value.shape[1], 128):
        parts = parts + value[:, start : start + 128]
    return jnp.broadcast_to(jnp.sum(parts, axis=1, keepdims=True), (value.shape[0], 128))


def in_lanes(values):
    lane = iota((OWN, 128), 1)
    row = jnp.zeros((OWN, 128), F32)
    for index, value in enumerate(values):
        row = jnp.where(lane == index, value, row)
    return row


def from_lanes(sums_ref, count):
    total = sums_ref[...]
    lane = iota((OWN, 128), 1)
    return [
        jnp.sum(jnp.where(lane == index, total, 0.0), axis=1, keepdims=True)
        for index in range(count)
    ]


def fetch(pairs, arrived):
    copies = [
        pltpu.make_async_copy(source, goal, arrived.at[index])
        for index, (source, goal) in enumerate(pairs)
    ]
    for copy in copies:
        copy.start()
    for copy in copies:
        copy.wait()


def sums_kernel(saved_hbm, upstream_hbm, sums_ref, saved_ref, upstream_ref, arrived):
    fetch(((saved_hbm, saved_ref), (upstream_hbm, upstream_ref)), arrived)
    saved = saved_ref[...].astype(F32)
    upstream = upstream_ref[...].astype(F32)
    sums_ref[...] = in_lanes(
        [
            lane_sum(saved),
            lane_sum(saved * saved),
            lane_sum(upstream),
            lane_sum(upstream * saved),
        ]
    )


def pack_kernel(acts_ref, packed_ref):
    for block in range(NY):
        start = block * BLOCK - REACH
        low, high = max(start, 0), min(start + SPAN, CELLS)
        packed_ref[block, :, low - start : high - start] = acts_ref[:, low:high]
        if low > start:
            packed_ref[block, :, : low - start] = jnp.zeros((OWN, low - start), BF16)
        if high < start + SPAN:
            packed_ref[block, :, high - start :] = jnp.zeros((OWN, start + SPAN - high), BF16)


def grad_kernel(
    counted,
    saved_hbm,
    upstream_hbm,
    sums_ref,
    params_ref,
    packed_ref,
    means_ref,
    saved_ref,
    upstream_ref,
    arrived,
):
    fetch(((saved_hbm, saved_ref), (upstream_hbm, upstream_ref)), arrived)
    saved_sum, square_sum, upstream_sum, product_sum = from_lanes(sums_ref, 4)
    mean = saved_sum / counted
    var = square_sum / counted - mean * mean
    inverse = lax.rsqrt(var + EPSILON)
    shift_grad = upstream_sum / counted
    gain_grad = (product_sum / counted - mean * shift_grad) * inverse
    means_ref[...] = in_lanes([gain_grad, shift_grad])
    scale = params_ref[2][:, :1] * inverse
    for block in range(NY):
        part = slice(block * BLOCK, (block + 1) * BLOCK)
        normed = (saved_ref[:, part].astype(F32) - mean) * inverse
        upstream = upstream_ref[:, part].astype(F32)
        grads = (scale * (upstream - shift_grad - normed * gain_grad)).astype(BF16)
        for to in range(NZ):
            packed_ref[block * NZ + to] = grads


def joined(parts_ref, block):
    whole = parts_ref[block, :, REACH : REACH + BLOCK].astype(F32)
    pieces = [whole[:, :384], whole[:, 384:REACH], whole[:, REACH:]]
    if block > 0:
        before = parts_ref[block - 1, :, REACH + BLOCK :].astype(F32)
        pieces[0] = pieces[0] + before[:, :384]
        pieces[1] = pieces[1] + before[:, 384:]
    if block < NY - 1:
        after = parts_ref[block + 1, :, :REACH].astype(F32)
        pieces[1] = pieces[1] + after[:, : REACH - 384]
        pieces[2] = pieces[2] + after[:, REACH - 384 :]
    return jnp.concatenate(pieces, axis=1)


def join_stats_kernel(half_ref, own_ref, other_ref, out_ref, sums_ref, held):
    held[...] = jnp.zeros_like(held)
    mine = half_ref[0] * HALF
    span = HALF + 2 * PLANE
    held[:, pl.ds(pl.multiple_of(mine, PLANE), span)] += own_ref[...]
    held[:, pl.ds(pl.multiple_of(HALF - mine, PLANE), span)] += other_ref[...]
    cells = held[:, PLANE : PLANE + CELLS]
    out_ref[...] = cells
    sums_ref[...] = in_lanes([lane_sum(cells), lane_sum(cells * cells)])


def join_kernel(parts_ref, out_ref):
    for block in range(NY):
        out_ref[:, block * BLOCK : (block + 1) * BLOCK] = joined(parts_ref, block).astype(BF16)


def relu_kernel(counted, conv_ref, sums_ref, params_ref, out_ref):
    first_sum, square_sum = from_lanes(sums_ref, 2)
    mean = first_sum / counted
    var = square_sum / counted - mean * mean
    scale = params_ref[0][:, :1] * lax.rsqrt(var + EPSILON)
    bias = params_ref[1][:, :1]
    out_ref[...] = jnp.maximum((conv_ref[...] - mean) * scale + bias, 0.0).astype(BF16)


def shaped(shape, dtype):
    return jax.ShapeDtypeStruct(shape, dtype)


def call(kernel, outs, specs, scratch=()):
    return pl.pallas_call(
        kernel,
        out_shape=outs,
        in_specs=specs,
        out_specs=jax.tree.map(lambda _: VMEM, outs),
        scratch_shapes=list(scratch),
        compiler_params=PARAMS,
        cost_estimate=pl.CostEstimate(flops=1000, bytes_accessed=1000, transcendentals=0),
    )


def exchange(value, axes):
    return lax.all_to_all(value, axes, 0, 0, tiled=True)


def shards(
    fwd_input,
    weight_one,
    gain_one,
    bias_one,
    saved_conv,
    cotangent,
    saved_input,
    weight_two,
    gain_two,
):
    y_axes = ("y_half", "y_rest")
    counted = lax.axis_size("vol") * CELLS
    half = lax.axis_index("y_half").astype(jnp.int32).reshape(1)
    base = (lax.axis_index(y_axes) * BLOCK).astype(jnp.int32).reshape(1)
    params = jnp.broadcast_to(
        jnp.stack([gain_one, bias_one, gain_two])[:, :, None], (3, OWN, 128)
    )
    saved, upstream = saved_conv[0], cotangent[0]
    fetched = [
        pltpu.VMEM((OWN, CELLS), BF16),
        pltpu.VMEM((OWN, CELLS), BF16),
        pltpu.SemaphoreType.DMA((2,)),
    ]
    hbm = pl.BlockSpec(memory_space=pl.ANY)

    cells = lax.all_gather(fwd_input[0].T, ("y_rest", "z"), axis=0, tiled=True)

    sums_two = call(sums_kernel, shaped((OWN, 128), F32), [hbm] * 2, fetched)(saved, upstream)
    acts = call(pack_kernel, shaped((NY, OWN, SPAN), BF16), [VMEM])(saved_input[0])
    acts = exchange(acts, y_axes)
    sums_two = lax.psum(sums_two, "vol")
    acts, sums_two = lax.optimization_barrier((acts, sums_two))
    acts = acts.reshape(GROUP, SPAN)

    packed, means = call(
        lambda *refs: grad_kernel(counted, *refs),
        (shaped((NY * NZ, OWN, BLOCK), BF16), shaped((OWN, 128), F32)),
        [hbm] * 2 + [VMEM] * 2,
        fetched,
    )(saved, upstream, sums_two, params)

    weight_one, weight_two, packed = lax.optimization_barrier((weight_one, weight_two, packed))
    grads = exchange(packed, (*y_axes, "z"))
    second = lax.all_gather(jnp.transpose(weight_two, (0, 2, 1)), y_axes, axis=0, tiled=False)
    across = lax.ppermute(weight_one, "y_half", [(0, 1), (1, 0)])
    first = jnp.concatenate([weight_one, across], axis=1).reshape(27 * 2 * OWN, CH)
    second = jnp.transpose(second, (1, 0, 2, 3)).reshape(ROWS, CH)
    grads, first, second = lax.optimization_barrier((grads, first, second))
    grads = grads.reshape(CH, BLOCK)

    filter_parts = call(
        filter_kernel,
        shaped((8, NY, GROUP, 128), BF16),
        [SMEM, VMEM, VMEM],
        [pltpu.VMEM((1024, BLOCK), BF16), pltpu.VMEM((CH, 1024), BF16)],
    )(base, grads, acts)
    second, filter_parts, cells = lax.optimization_barrier((second, filter_parts, cells))
    filter_parts = exchange(filter_parts.reshape(8 * NY, GROUP, 128), ("vol", *y_axes))
    input_parts = call(
        backward_kernel,
        shaped((NY, OWN, SPAN), BF16),
        [SMEM, VMEM, VMEM],
        [pltpu.VMEM((ROWS, BLOCK), F32)],
    )(base, second, grads)
    first, input_parts = lax.optimization_barrier((first, input_parts))
    input_parts = exchange(input_parts, y_axes)

    span = HALF + 2 * PLANE
    own, other = call(
        forward_kernel,
        (shaped((OWN, span), F32), shaped((OWN, span), F32)),
        [VMEM, VMEM],
        [pltpu.VMEM((27 * 2 * OWN, HALF), F32), pltpu.VMEM((2 * OWN, span), F32)],
    )(first, cells)
    other = lax.ppermute(other, "y_half", [(0, 1), (1, 0)])
    conv_out, sums_one = call(
        join_stats_kernel,
        (shaped((OWN, CELLS), F32), shaped((OWN, 128), F32)),
        [SMEM, VMEM, VMEM],
        [pltpu.VMEM((OWN, CELLS + 2 * PLANE), F32)],
    )(half, own, other)
    sums_one = lax.psum(sums_one, "vol")
    activation = call(
        lambda *refs: relu_kernel(counted, *refs), shaped((OWN, CELLS), BF16), [VMEM] * 3
    )(conv_out, sums_one, params)
    input_grad = call(join_kernel, shaped((OWN, CELLS), BF16), [VMEM])(input_parts)

    summed = jnp.sum(filter_parts.astype(F32), axis=0) / math.sqrt(counted)
    weight_grad = jnp.transpose(summed[:, : 27 * OWN].reshape(GROUP, 27, OWN), (1, 0, 2))
    return (activation[None], input_grad[None], weight_grad, means[:, 0], means[:, 1])


def solution(mesh):
    names = ("vol", "y_half", "y_rest", "z")
    cut = Mesh(mesh.devices.reshape(mesh.devices.shape[0], 2, NY // 2, NZ), names)
    chan = names[1:]
    return jax.shard_map(
        shards,
        mesh=cut,
        in_specs=(
            P("vol", None, chan),
            P(None, chan, None),
            P(chan),
            P(chan),
            P("vol", chan, None),
            P("vol", chan, None),
            P("vol", chan, None),
            P(None, None, chan),
            P(chan),
        ),
        out_specs=(
            P("vol", chan, None),
            P("vol", chan, None),
            P(None, "vol", chan),
            P(chan),
            P(chan),
        ),
        check_vma=False,
    )
```

```python
import math

import jax
import jax.numpy as jnp
from jax import lax
from jax.experimental import pallas as pl
from jax.experimental.pallas import tpu as pltpu
from jax.sharding import Mesh
from jax.sharding import PartitionSpec as P

PLANE = 1024
BLOCK = 1536
EDGE = 128
REACH = PLANE + EDGE
SPAN = BLOCK + 2 * REACH
CELLS = 12288
NY = 8
NZ = 8
OWN = 4
GROUP = NY * OWN
CH = 256
ROWS = 27 * GROUP
EPSILON = 1e-05
F32 = jnp.float32
BF16 = jnp.bfloat16

VMEM = pl.BlockSpec(memory_space=pltpu.VMEM)
SMEM = pl.BlockSpec(memory_space=pltpu.SMEM)
PARAMS = pltpu.CompilerParams(vmem_limit_bytes=40 * 1024 * 1024)


def iota(shape, axis):
    return lax.broadcasted_iota(jnp.int32, shape, axis)


def shift(value, amount):
    lanes = value.shape[1]
    return pltpu.roll(value, (-amount) % lanes, 1)


def nt_dot(left, right):
    return lax.dot_general(left, right, (((1,), (1,)), ((), ())), preferred_element_type=F32)


def spread(base, terms, out_ref, sign):
    def rows(group, carry):
        lane = iota((8, BLOCK), 1)
        along_x = lane & 31
        along_y = lax.shift_right_logical(lane + base, 5) & 31
        ends = {1: along_x >= 1, -1: along_x <= 30}
        sides = {1: along_y >= 1, -1: along_y <= 30}
        margin = jnp.zeros((8, EDGE), F32)
        by_plane = {}
        for a in (-1, 0, 1):
            total = None
            for b in (-1, 0, 1):
                line = None
                for c in (-1, 0, 1):
                    index = 9 * (a + 1) + 3 * (b + 1) + (c + 1)
                    term = terms[pl.ds(pl.multiple_of(index * GROUP + group * 8, 8), 8), :]
                    if c != 0:
                        term = shift(jnp.where(ends[sign * c], term, 0.0), sign * c)
                    line = term if line is None else line + term
                if b != 0:
                    line = jnp.where(sides[sign * b], line, 0.0)
                line = jnp.concatenate([margin, line, margin], axis=1)
                if b != 0:
                    line = shift(line, sign * b * 32)
                total = line if total is None else total + line
            by_plane[sign * a] = total
        low, mid, high = by_plane[1], by_plane[0], by_plane[-1]
        pieces = (
            (0, low[:, :1024]),
            (1024, low[:, 1024:] + mid[:, :768]),
            (1792, mid[:, 768:1024]),
            (2048, mid[:, 1024:] + high[:, :768]),
            (2816, high[:, 768:]),
        )
        for start, piece in pieces:
            stop = start + piece.shape[1]
            out_ref[2 * group, :, start:stop] = piece[:OWN].astype(out_ref.dtype)
            out_ref[2 * group + 1, :, start:stop] = piece[OWN:].astype(out_ref.dtype)
        return carry

    lax.fori_loop(0, GROUP // 8, rows, 0)


def forward_kernel(base_ref, weight_ref, cells_ref, out_ref, terms):
    def columns(step, carry):
        part = pl.ds(pl.multiple_of(step * 256, 256), 256)
        terms[:, part] = nt_dot(weight_ref[...], cells_ref[part, :])
        return carry

    lax.fori_loop(0, BLOCK // 256, columns, 0)
    spread(base_ref[0], terms, out_ref, 1)


def backward_kernel(base_ref, weight_ref, grads_ref, out_ref, terms):
    def columns(step, carry):
        part = pl.ds(pl.multiple_of(step * 256, 256), 256)
        terms[:, part] = jnp.dot(
            weight_ref[...], grads_ref[:, part], preferred_element_type=F32
        )
        return carry

    lax.fori_loop(0, BLOCK // 256, columns, 0)
    spread(base_ref[0], terms, out_ref, -1)


def filter_kernel(base_ref, grads_ref, acts_ref, out_ref, copies, product):
    base = base_ref[0]

    def rows(group, carry):
        lane = iota((16, SPAN), 1)
        along_x = lane & 31
        along_y = lax.shift_right_logical(lane + (base + 2 * PLANE - REACH), 5) & 31
        first = pl.multiple_of(group * 16, 16)
        acts = acts_ref[pl.ds(first, 16), :].astype(F32)
        ends = {1: along_x <= 30, -1: along_x >= 1}
        sides = {1: along_y <= 30, -1: along_y >= 1}
        for b in (-1, 0, 1):
            for c in (-1, 0, 1):
                moved = acts
                if b != 0 or c != 0:
                    moved = shift(acts, 32 * b + c)
                if c != 0:
                    moved = jnp.where(ends[c], moved, 0.0)
                if b != 0:
                    moved = jnp.where(sides[b], moved, 0.0)
                moved = moved.astype(BF16)
                for a in (-1, 0, 1):
                    index = 9 * (a + 1) + 3 * (b + 1) + (c + 1)
                    start = REACH + PLANE * a
                    copies[pl.ds(index * GROUP + first, 16), :] = moved[:, start : start + BLOCK]
        return carry

    lax.fori_loop(0, GROUP // 16, rows, 0)
    copies[ROWS:, :] = jnp.zeros((1024 - ROWS, BLOCK), BF16)

    def offsets(step, carry):
        part = pl.ds(pl.multiple_of(step * 256, 256), 256)
        product[:, part] = nt_dot(grads_ref[...], copies[part, :]).astype(BF16)
        return carry

    lax.fori_loop(0, 4, offsets, 0)

    def owners(step, carry):
        of = iota((1024, 256), 0)
        to = iota((1024, 256), 1)
        same = (
            (2 * step + lax.shift_right_logical(to, 7)) == (lax.shift_right_logical(of, 2) & 7)
        ) & ((to & 127) == (lax.shift_right_logical(of, 5) * 4 + (of & 3)))
        select = jnp.where(same, 1.0, 0.0).astype(BF16)
        placed = jnp.dot(product[...], select, preferred_element_type=F32).astype(BF16)
        for vol in range(8):
            for half in range(2):
                out_ref[vol, 2 * step + half] = placed[
                    32 * vol : 32 * vol + 32, 128 * half : 128 * half + 128
                ]
        return carry

    lax.fori_loop(0, 4, owners, 0)


def lane_sum(value):
    parts = value[:, :128]
    for start in range(128, value.shape[1], 128):
        parts = parts + value[:, start : start + 128]
    return jnp.broadcast_to(jnp.sum(parts, axis=1, keepdims=True), (value.shape[0], 128))


def in_lanes(values):
    lane = iota((OWN, 128), 1)
    row = jnp.zeros((OWN, 128), F32)
    for index, value in enumerate(values):
        row = jnp.where(lane == index, value, row)
    return row


def from_lanes(sums_ref, count):
    total = sums_ref[...]
    lane = iota((OWN, 128), 1)
    return [
        jnp.sum(jnp.where(lane == index, total, 0.0), axis=1, keepdims=True)
        for index in range(count)
    ]


def sums_kernel(saved_ref, upstream_ref, sums_ref):
    saved = saved_ref[...].astype(F32)
    upstream = upstream_ref[...].astype(F32)
    sums_ref[...] = in_lanes(
        [
            lane_sum(saved),
            lane_sum(saved * saved),
            lane_sum(upstream),
            lane_sum(upstream * saved),
        ]
    )


def pack_kernel(acts_ref, packed_ref):
    for block in range(NY):
        start = block * BLOCK - REACH
        low, high = max(start, 0), min(start + SPAN, CELLS)
        packed_ref[block, :, low - start : high - start] = acts_ref[:, low:high]
        if low > start:
            packed_ref[block, :, : low - start] = jnp.zeros((OWN, low - start), BF16)
        if high < start + SPAN:
            packed_ref[block, :, high - start :] = jnp.zeros((OWN, start + SPAN - high), BF16)


def grad_kernel(counted, saved_ref, upstream_ref, sums_ref, params_ref, packed_ref, means_ref):
    saved_sum, square_sum, upstream_sum, product_sum = from_lanes(sums_ref, 4)
    mean = saved_sum / counted
    var = square_sum / counted - mean * mean
    inverse = lax.rsqrt(var + EPSILON)
    shift_grad = upstream_sum / counted
    gain_grad = (product_sum / counted - mean * shift_grad) * inverse
    means_ref[...] = in_lanes([gain_grad, shift_grad])
    scale = params_ref[2][:, :1] * inverse
    for block in range(NY):
        part = slice(block * BLOCK, (block + 1) * BLOCK)
        normed = (saved_ref[:, part].astype(F32) - mean) * inverse
        upstream = upstream_ref[:, part].astype(F32)
        grads = (scale * (upstream - shift_grad - normed * gain_grad)).astype(BF16)
        for to in range(NZ):
            packed_ref[block * NZ + to] = grads


def joined(parts_ref, block):
    whole = parts_ref[block, :, REACH : REACH + BLOCK].astype(F32)
    pieces = [whole[:, :384], whole[:, 384:REACH], whole[:, REACH:]]
    if block > 0:
        before = parts_ref[block - 1, :, REACH + BLOCK :].astype(F32)
        pieces[0] = pieces[0] + before[:, :384]
        pieces[1] = pieces[1] + before[:, 384:]
    if block < NY - 1:
        after = parts_ref[block + 1, :, :REACH].astype(F32)
        pieces[1] = pieces[1] + after[:, : REACH - 384]
        pieces[2] = pieces[2] + after[:, REACH - 384 :]
    return jnp.concatenate(pieces, axis=1)


def join_stats_kernel(parts_ref, out_ref, sums_ref):
    total = jnp.zeros((OWN, 128), F32)
    squares = jnp.zeros((OWN, 128), F32)
    for block in range(NY):
        cells = joined(parts_ref, block)
        out_ref[:, block * BLOCK : (block + 1) * BLOCK] = cells
        total = total + lane_sum(cells)
        squares = squares + lane_sum(cells * cells)
    sums_ref[...] = in_lanes([total, squares])


def join_kernel(parts_ref, out_ref):
    for block in range(NY):
        out_ref[:, block * BLOCK : (block + 1) * BLOCK] = joined(parts_ref, block).astype(BF16)


def relu_kernel(counted, conv_ref, sums_ref, params_ref, out_ref):
    first_sum, square_sum = from_lanes(sums_ref, 2)
    mean = first_sum / counted
    var = square_sum / counted - mean * mean
    scale = params_ref[0][:, :1] * lax.rsqrt(var + EPSILON)
    bias = params_ref[1][:, :1]
    out_ref[...] = jnp.maximum((conv_ref[...] - mean) * scale + bias, 0.0).astype(BF16)


def shaped(shape, dtype):
    return jax.ShapeDtypeStruct(shape, dtype)


def call(kernel, outs, specs, scratch=()):
    return pl.pallas_call(
        kernel,
        out_shape=outs,
        in_specs=specs,
        out_specs=jax.tree.map(lambda _: VMEM, outs),
        scratch_shapes=list(scratch),
        compiler_params=PARAMS,
        cost_estimate=pl.CostEstimate(flops=1000, bytes_accessed=1000, transcendentals=0),
    )


def exchange(value, axes):
    return lax.all_to_all(value, axes, 0, 0, tiled=True)


def gathered(filters):
    filters = lax.all_gather(filters, "y", axis=0, tiled=False)
    return jnp.transpose(filters, (1, 0, 2, 3)).reshape(ROWS, CH)


def shards(
    fwd_input,
    weight_one,
    gain_one,
    bias_one,
    saved_conv,
    cotangent,
    saved_input,
    weight_two,
    gain_two,
):
    counted = lax.axis_size("vol") * CELLS
    base = (lax.axis_index("y") * BLOCK).astype(jnp.int32).reshape(1)
    params = jnp.broadcast_to(
        jnp.stack([gain_one, bias_one, gain_two])[:, :, None], (3, OWN, 128)
    )
    saved, upstream = saved_conv[0], cotangent[0]

    sums_two = call(sums_kernel, shaped((OWN, 128), F32), [VMEM] * 2)(saved, upstream)
    acts = call(pack_kernel, shaped((NY, OWN, SPAN), BF16), [VMEM])(saved_input[0])
    acts = exchange(acts, "y")
    sums_two = lax.psum(sums_two, "vol")
    acts, sums_two = lax.optimization_barrier((acts, sums_two))
    acts = acts.reshape(GROUP, SPAN)
    packed, means = call(
        lambda *refs: grad_kernel(counted, *refs),
        (shaped((NY * NZ, OWN, BLOCK), BF16), shaped((OWN, 128), F32)),
        [VMEM] * 4,
    )(saved, upstream, sums_two, params)

    cells, packed = lax.optimization_barrier((fwd_input[0].T, packed))
    grads = exchange(packed, ("y", "z"))
    cells = lax.all_gather(cells, "z", axis=0, tiled=True)
    grads, cells = lax.optimization_barrier((grads, cells))
    grads = grads.reshape(CH, BLOCK)
    filter_parts = call(
        filter_kernel,
        shaped((8, NY, GROUP, 128), BF16),
        [SMEM, VMEM, VMEM],
        [pltpu.VMEM((1024, BLOCK), BF16), pltpu.VMEM((CH, 1024), BF16)],
    )(base, grads, acts)

    first, filter_parts = lax.optimization_barrier((weight_one, filter_parts))
    filter_parts = exchange(filter_parts.reshape(8 * NY, GROUP, 128), ("vol", "y"))
    first = gathered(first)
    conv_parts = call(
        forward_kernel,
        shaped((NY, OWN, SPAN), F32),
        [SMEM, VMEM, VMEM],
        [pltpu.VMEM((ROWS, BLOCK), F32)],
    )(base, first, cells)

    second, conv_parts, filter_parts = lax.optimization_barrier(
        (weight_two, conv_parts, filter_parts)
    )
    conv_parts = exchange(conv_parts, "y")
    second = gathered(jnp.transpose(second, (0, 2, 1)))
    input_parts = call(
        backward_kernel,
        shaped((NY, OWN, SPAN), BF16),
        [SMEM, VMEM, VMEM],
        [pltpu.VMEM((ROWS, BLOCK), F32)],
    )(base, second, grads)

    conv_parts, input_parts = lax.optimization_barrier((conv_parts, input_parts))
    input_parts = exchange(input_parts, "y")
    conv_out, sums_one = call(
        join_stats_kernel, (shaped((OWN, CELLS), F32), shaped((OWN, 128), F32)), [VMEM]
    )(conv_parts)
    sums_one = lax.psum(sums_one, "vol")
    activation = call(
        lambda *refs: relu_kernel(counted, *refs), shaped((OWN, CELLS), BF16), [VMEM] * 3
    )(conv_out, sums_one, params)
    input_grad = call(join_kernel, shaped((OWN, CELLS), BF16), [VMEM])(input_parts)

    summed = jnp.sum(filter_parts.astype(F32), axis=0) / math.sqrt(counted)
    weight_grad = jnp.transpose(summed[:, : 27 * OWN].reshape(GROUP, 27, OWN), (1, 0, 2))
    return (activation[None], input_grad[None], weight_grad, means[:, 0], means[:, 1])


def solution(mesh):
    cut = Mesh(mesh.devices.reshape(mesh.devices.shape[0], NY, NZ), ("vol", "y", "z"))
    chan = ("y", "z")
    return jax.shard_map(
        shards,
        mesh=cut,
        in_specs=(
            P("vol", None, chan),
            P(None, chan, None),
            P(chan),
            P(chan),
            P("vol", chan, None),
            P("vol", chan, None),
            P("vol", chan, None),
            P(None, None, chan),
            P(chan),
        ),
        out_specs=(
            P("vol", chan, None),
            P("vol", chan, None),
            P(None, "vol", chan),
            P(chan),
            P(chan),
        ),
        check_vma=False,
    )
```

```python
import math

import jax
import jax.numpy as jnp
from jax import lax
from jax.experimental import pallas as pl
from jax.experimental.pallas import tpu as pltpu
from jax.sharding import Mesh
from jax.sharding import PartitionSpec as P

PLANE = 1024
BLOCK = 1536
EDGE = 128
REACH = PLANE + EDGE
SPAN = BLOCK + 2 * REACH
CELLS = 12288
HALF = 6
NY = 8
NZ = 8
OWN = 4
GROUP = NY * OWN
CH = 256
ROWS = 27 * GROUP
EPSILON = 1e-05
F32 = jnp.float32
BF16 = jnp.bfloat16

VMEM = pl.BlockSpec(memory_space=pltpu.VMEM)
SMEM = pl.BlockSpec(memory_space=pltpu.SMEM)
PARAMS = pltpu.CompilerParams(vmem_limit_bytes=40 * 1024 * 1024)


def iota(shape, axis):
    return lax.broadcasted_iota(jnp.int32, shape, axis)


def shift(value, amount):
    lanes = value.shape[1]
    return pltpu.roll(value, (-amount) % lanes, 1)


def nt_dot(left, right):
    return lax.dot_general(left, right, (((1,), (1,)), ((), ())), preferred_element_type=F32)


def spread(base, terms, out_ref, sign):
    def rows(group, carry):
        lane = iota((8, BLOCK), 1)
        along_x = lane & 31
        along_y = lax.shift_right_logical(lane + base, 5) & 31
        ends = {1: along_x >= 1, -1: along_x <= 30}
        sides = {1: along_y >= 1, -1: along_y <= 30}
        margin = jnp.zeros((8, EDGE), F32)
        by_plane = {}
        for a in (-1, 0, 1):
            total = None
            for b in (-1, 0, 1):
                line = None
                for c in (-1, 0, 1):
                    index = 9 * (a + 1) + 3 * (b + 1) + (c + 1)
                    term = terms[pl.ds(pl.multiple_of(index * GROUP + group * 8, 8), 8), :]
                    if c != 0:
                        term = shift(jnp.where(ends[sign * c], term, 0.0), sign * c)
                    line = term if line is None else line + term
                if b != 0:
                    line = jnp.where(sides[sign * b], line, 0.0)
                line = jnp.concatenate([margin, line, margin], axis=1)
                if b != 0:
                    line = shift(line, sign * b * 32)
                total = line if total is None else total + line
            by_plane[sign * a] = total
        low, mid, high = by_plane[1], by_plane[0], by_plane[-1]
        pieces = (
            (0, low[:, :1024]),
            (1024, low[:, 1024:] + mid[:, :768]),
            (1792, mid[:, 768:1024]),
            (2048, mid[:, 1024:] + high[:, :768]),
            (2816, high[:, 768:]),
        )
        for start, piece in pieces:
            stop = start + piece.shape[1]
            out_ref[2 * group, :, start:stop] = piece[:OWN].astype(out_ref.dtype)
            out_ref[2 * group + 1, :, start:stop] = piece[OWN:].astype(out_ref.dtype)
        return carry

    lax.fori_loop(0, GROUP // 8, rows, 0)


def forward_kernel(low_ref, high_ref, lower_ref, upper_ref, out_ref, sums_ref, terms, held):
    at = pl.program_id(0)

    @pl.when(at == 0)
    def _():
        held[...] = jnp.zeros_like(held)

    def columns(step, carry):
        part = pl.ds(pl.multiple_of(step * 256, 256), 256)
        terms[:, part] = nt_dot(low_ref[...], lower_ref[part, :]) + nt_dot(
            high_ref[...], upper_ref[part, :]
        )
        return carry

    lax.fori_loop(0, PLANE // 256, columns, 0)
    lane = iota((8, PLANE), 1)
    along_x, along_y = lane & 31, lax.shift_right_logical(lane, 5)
    ends = {1: along_x >= 1, -1: along_x <= 30}
    sides = {1: along_y >= 1, -1: along_y <= 30}
    for a in (-1, 0, 1):
        total = None
        for b in (-1, 0, 1):
            line = None
            for c in (-1, 0, 1):
                index = 9 * (a + 1) + 3 * (b + 1) + (c + 1)
                term = terms[8 * index : 8 * index + 8, :]
                if c != 0:
                    term = shift(jnp.where(ends[c], term, 0.0), c)
                line = term if line is None else line + term
            if b != 0:
                line = shift(jnp.where(sides[b], line, 0.0), 32 * b)
            total = line if total is None else total + line
        goal = pl.ds(pl.multiple_of((at + 1 - a) * PLANE, PLANE), PLANE)
        held[:, goal] += total

    @pl.when(at == HALF - 1)
    def _():
        total = jnp.zeros((OWN, 128), F32)
        squares = jnp.zeros((OWN, 128), F32)
        for z in range(2 * HALF):
            side, own = divmod(z, HALF)
            cells = held[OWN * side : OWN * side + OWN, (own + 1) * PLANE : (own + 2) * PLANE]
            if z == HALF - 1:
                cells = cells + held[OWN:, :PLANE]
            if z == HALF:
                cells = cells + held[:OWN, (HALF + 1) * PLANE :]
            out_ref[:, z * PLANE : (z + 1) * PLANE] = cells
            total = total + lane_sum(cells)
            squares = squares + lane_sum(cells * cells)
        sums_ref[...] = in_lanes([total, squares])


def backward_kernel(base_ref, weight_ref, grads_ref, out_ref, terms):
    def columns(step, carry):
        part = pl.ds(pl.multiple_of(step * 256, 256), 256)
        terms[:, part] = jnp.dot(
            weight_ref[...], grads_ref[:, part], preferred_element_type=F32
        )
        return carry

    lax.fori_loop(0, BLOCK // 256, columns, 0)
    spread(base_ref[0], terms, out_ref, -1)


def filter_kernel(base_ref, grads_ref, acts_ref, out_ref, copies, product):
    base = base_ref[0]

    def rows(group, carry):
        lane = iota((16, SPAN), 1)
        along_x = lane & 31
        along_y = lax.shift_right_logical(lane + (base + 2 * PLANE - REACH), 5) & 31
        first = pl.multiple_of(group * 16, 16)
        acts = acts_ref[pl.ds(first, 16), :].astype(F32)
        ends = {1: along_x <= 30, -1: along_x >= 1}
        sides = {1: along_y <= 30, -1: along_y >= 1}
        for b in (-1, 0, 1):
            for c in (-1, 0, 1):
                moved = acts
                if b != 0 or c != 0:
                    moved = shift(acts, 32 * b + c)
                if c != 0:
                    moved = jnp.where(ends[c], moved, 0.0)
                if b != 0:
                    moved = jnp.where(sides[b], moved, 0.0)
                moved = moved.astype(BF16)
                for a in (-1, 0, 1):
                    index = 9 * (a + 1) + 3 * (b + 1) + (c + 1)
                    start = REACH + PLANE * a
                    copies[pl.ds(index * GROUP + first, 16), :] = moved[:, start : start + BLOCK]
        return carry

    lax.fori_loop(0, GROUP // 16, rows, 0)
    copies[ROWS:, :] = jnp.zeros((1024 - ROWS, BLOCK), BF16)

    def offsets(step, carry):
        part = pl.ds(pl.multiple_of(step * 256, 256), 256)
        product[:, part] = nt_dot(grads_ref[...], copies[part, :]).astype(BF16)
        return carry

    lax.fori_loop(0, 4, offsets, 0)

    def owners(step, carry):
        of = iota((1024, 256), 0)
        to = iota((1024, 256), 1)
        same = (
            (2 * step + lax.shift_right_logical(to, 7)) == (lax.shift_right_logical(of, 2) & 7)
        ) & ((to & 127) == (lax.shift_right_logical(of, 5) * 4 + (of & 3)))
        select = jnp.where(same, 1.0, 0.0).astype(BF16)
        placed = jnp.dot(product[...], select, preferred_element_type=F32).astype(BF16)
        for vol in range(8):
            for half in range(2):
                out_ref[vol, 2 * step + half] = placed[
                    32 * vol : 32 * vol + 32, 128 * half : 128 * half + 128
                ]
        return carry

    lax.fori_loop(0, 4, owners, 0)


def lane_sum(value):
    parts = value[:, :128]
    for start in range(128, value.shape[1], 128):
        parts = parts + value[:, start : start + 128]
    return jnp.broadcast_to(jnp.sum(parts, axis=1, keepdims=True), (value.shape[0], 128))


def in_lanes(values):
    lane = iota((OWN, 128), 1)
    row = jnp.zeros((OWN, 128), F32)
    for index, value in enumerate(values):
        row = jnp.where(lane == index, value, row)
    return row


def from_lanes(sums_ref, count):
    total = sums_ref[...]
    lane = iota((OWN, 128), 1)
    return [
        jnp.sum(jnp.where(lane == index, total, 0.0), axis=1, keepdims=True)
        for index in range(count)
    ]


def sums_kernel(saved_ref, upstream_ref, sums_ref):
    saved = saved_ref[...].astype(F32)
    upstream = upstream_ref[...].astype(F32)
    sums_ref[...] = in_lanes(
        [
            lane_sum(saved),
            lane_sum(saved * saved),
            lane_sum(upstream),
            lane_sum(upstream * saved),
        ]
    )


def pack_kernel(acts_ref, packed_ref):
    for block in range(NY):
        start = block * BLOCK - REACH
        low, high = max(start, 0), min(start + SPAN, CELLS)
        packed_ref[block, :, low - start : high - start] = acts_ref[:, low:high]
        if low > start:
            packed_ref[block, :, : low - start] = jnp.zeros((OWN, low - start), BF16)
        if high < start + SPAN:
            packed_ref[block, :, high - start :] = jnp.zeros((OWN, start + SPAN - high), BF16)


def grad_kernel(counted, saved_ref, upstream_ref, sums_ref, params_ref, packed_ref, means_ref):
    saved_sum, square_sum, upstream_sum, product_sum = from_lanes(sums_ref, 4)
    mean = saved_sum / counted
    var = square_sum / counted - mean * mean
    inverse = lax.rsqrt(var + EPSILON)
    shift_grad = upstream_sum / counted
    gain_grad = (product_sum / counted - mean * shift_grad) * inverse
    means_ref[...] = in_lanes([gain_grad, shift_grad])
    scale = params_ref[2][:, :1] * inverse
    for block in range(NY):
        part = slice(block * BLOCK, (block + 1) * BLOCK)
        normed = (saved_ref[:, part].astype(F32) - mean) * inverse
        upstream = upstream_ref[:, part].astype(F32)
        grads = (scale * (upstream - shift_grad - normed * gain_grad)).astype(BF16)
        for to in range(NZ):
            packed_ref[block * NZ + to] = grads


def joined(parts_ref, block):
    whole = parts_ref[block, :, REACH : REACH + BLOCK].astype(F32)
    pieces = [whole[:, :384], whole[:, 384:REACH], whole[:, REACH:]]
    if block > 0:
        before = parts_ref[block - 1, :, REACH + BLOCK :].astype(F32)
        pieces[0] = pieces[0] + before[:, :384]
        pieces[1] = pieces[1] + before[:, 384:]
    if block < NY - 1:
        after = parts_ref[block + 1, :, :REACH].astype(F32)
        pieces[1] = pieces[1] + after[:, : REACH - 384]
        pieces[2] = pieces[2] + after[:, REACH - 384 :]
    return jnp.concatenate(pieces, axis=1)


def join_kernel(parts_ref, out_ref):
    for block in range(NY):
        out_ref[:, block * BLOCK : (block + 1) * BLOCK] = joined(parts_ref, block).astype(BF16)


def relu_kernel(counted, conv_ref, sums_ref, params_ref, out_ref):
    first_sum, square_sum = from_lanes(sums_ref, 2)
    mean = first_sum / counted
    var = square_sum / counted - mean * mean
    scale = params_ref[0][:, :1] * lax.rsqrt(var + EPSILON)
    bias = params_ref[1][:, :1]
    out_ref[...] = jnp.maximum((conv_ref[...] - mean) * scale + bias, 0.0).astype(BF16)


def shaped(shape, dtype):
    return jax.ShapeDtypeStruct(shape, dtype)


def call(kernel, outs, specs, scratch=()):
    return pl.pallas_call(
        kernel,
        out_shape=outs,
        in_specs=specs,
        out_specs=jax.tree.map(lambda _: VMEM, outs),
        scratch_shapes=list(scratch),
        compiler_params=PARAMS,
        cost_estimate=pl.CostEstimate(flops=1000, bytes_accessed=1000, transcendentals=0),
    )


def exchange(value, axes):
    return lax.all_to_all(value, axes, 0, 0, tiled=True)


def gathered(filters):
    filters = lax.all_gather(filters, "y", axis=0, tiled=False)
    return jnp.transpose(filters, (1, 0, 2, 3)).reshape(ROWS, CH)


def shards(
    fwd_input,
    weight_one,
    gain_one,
    bias_one,
    saved_conv,
    cotangent,
    saved_input,
    weight_two,
    gain_two,
):
    counted = lax.axis_size("vol") * CELLS
    base = (lax.axis_index("y") * BLOCK).astype(jnp.int32).reshape(1)
    params = jnp.broadcast_to(
        jnp.stack([gain_one, bias_one, gain_two])[:, :, None], (3, OWN, 128)
    )
    saved, upstream = saved_conv[0], cotangent[0]

    cells = lax.all_gather(fwd_input[0].T, ("y", "z"), axis=0, tiled=True)
    low = jnp.pad(weight_one, ((0, 0), (0, OWN), (0, 0))).reshape(27 * 2 * OWN, CH)
    high = jnp.pad(weight_one, ((0, 0), (OWN, 0), (0, 0))).reshape(27 * 2 * OWN, CH)

    sums_two = call(sums_kernel, shaped((OWN, 128), F32), [VMEM] * 2)(saved, upstream)
    acts = call(pack_kernel, shaped((NY, OWN, SPAN), BF16), [VMEM])(saved_input[0])
    acts = exchange(acts, "y")
    sums_two = lax.psum(sums_two, "vol")
    acts, sums_two = lax.optimization_barrier((acts, sums_two))
    acts = acts.reshape(GROUP, SPAN)
    packed, means = call(
        lambda *refs: grad_kernel(counted, *refs),
        (shaped((NY * NZ, OWN, BLOCK), BF16), shaped((OWN, 128), F32)),
        [VMEM] * 4,
    )(saved, upstream, sums_two, params)

    second, packed = lax.optimization_barrier((weight_two, packed))
    grads = exchange(packed, ("y", "z"))
    second = gathered(jnp.transpose(second, (0, 2, 1)))
    grads, second = lax.optimization_barrier((grads, second))
    grads = grads.reshape(CH, BLOCK)
    filter_parts = call(
        filter_kernel,
        shaped((8, NY, GROUP, 128), BF16),
        [SMEM, VMEM, VMEM],
        [pltpu.VMEM((1024, BLOCK), BF16), pltpu.VMEM((CH, 1024), BF16)],
    )(base, grads, acts)
    second, filter_parts = lax.optimization_barrier((second, filter_parts))
    filter_parts = exchange(filter_parts.reshape(8 * NY, GROUP, 128), ("vol", "y"))
    input_parts = call(
        backward_kernel,
        shaped((NY, OWN, SPAN), BF16),
        [SMEM, VMEM, VMEM],
        [pltpu.VMEM((ROWS, BLOCK), F32)],
    )(base, second, grads)

    cells, input_parts = lax.optimization_barrier((cells, input_parts))
    input_parts = exchange(input_parts, "y")
    conv_out, sums_one = pl.pallas_call(
        forward_kernel,
        out_shape=(shaped((OWN, CELLS), F32), shaped((OWN, 128), F32)),
        grid=(HALF,),
        in_specs=[
            pl.BlockSpec((27 * 2 * OWN, CH), lambda at: (0, 0)),
            pl.BlockSpec((27 * 2 * OWN, CH), lambda at: (0, 0)),
            pl.BlockSpec((PLANE, CH), lambda at: (at, 0)),
            pl.BlockSpec((PLANE, CH), lambda at: (at + HALF, 0)),
        ],
        out_specs=(
            pl.BlockSpec((OWN, CELLS), lambda at: (0, 0)),
            pl.BlockSpec((OWN, 128), lambda at: (0, 0)),
        ),
        scratch_shapes=[
            pltpu.VMEM((27 * 2 * OWN, PLANE), F32),
            pltpu.VMEM((2 * OWN, (HALF + 2) * PLANE), F32),
        ],
        compiler_params=PARAMS,
        cost_estimate=pl.CostEstimate(flops=1000, bytes_accessed=1000, transcendentals=0),
    )(low, high, cells, cells)
    sums_one = lax.psum(sums_one, "vol")
    activation = call(
        lambda *refs: relu_kernel(counted, *refs), shaped((OWN, CELLS), BF16), [VMEM] * 3
    )(conv_out, sums_one, params)
    input_grad = call(join_kernel, shaped((OWN, CELLS), BF16), [VMEM])(input_parts)

    summed = jnp.sum(filter_parts.astype(F32), axis=0) / math.sqrt(counted)
    weight_grad = jnp.transpose(summed[:, : 27 * OWN].reshape(GROUP, 27, OWN), (1, 0, 2))
    return (activation[None], input_grad[None], weight_grad, means[:, 0], means[:, 1])


def solution(mesh):
    cut = Mesh(mesh.devices.reshape(mesh.devices.shape[0], NY, NZ), ("vol", "y", "z"))
    chan = ("y", "z")
    return jax.shard_map(
        shards,
        mesh=cut,
        in_specs=(
            P("vol", None, chan),
            P(None, chan, None),
            P(chan),
            P(chan),
            P("vol", chan, None),
            P("vol", chan, None),
            P("vol", chan, None),
            P(None, None, chan),
            P(chan),
        ),
        out_specs=(
            P("vol", chan, None),
            P("vol", chan, None),
            P(None, "vol", chan),
            P(chan),
            P(chan),
        ),
        check_vma=False,
    )
```

```python
import math

import jax
import jax.numpy as jnp
from jax import lax
from jax.experimental import pallas as pl
from jax.experimental.pallas import tpu as pltpu
from jax.sharding import Mesh
from jax.sharding import PartitionSpec as P

PLANE = 1024
BLOCK = 1536
EDGE = 128
REACH = PLANE + EDGE
SPAN = BLOCK + 2 * REACH
CELLS = 12288
HALF = 6
NY = 8
NZ = 8
OWN = 4
GROUP = NY * OWN
CH = 256
ROWS = 27 * GROUP
EPSILON = 1e-05
F32 = jnp.float32
BF16 = jnp.bfloat16

VMEM = pl.BlockSpec(memory_space=pltpu.VMEM)
SMEM = pl.BlockSpec(memory_space=pltpu.SMEM)
PARAMS = pltpu.CompilerParams(vmem_limit_bytes=40 * 1024 * 1024)


def iota(shape, axis):
    return lax.broadcasted_iota(jnp.int32, shape, axis)


def shift(value, amount):
    lanes = value.shape[1]
    return pltpu.roll(value, (-amount) % lanes, 1)


def nt_dot(left, right):
    return lax.dot_general(left, right, (((1,), (1,)), ((), ())), preferred_element_type=F32)


def spread(base, terms, out_ref, sign):
    def rows(group, carry):
        lane = iota((8, BLOCK), 1)
        along_x = lane & 31
        along_y = lax.shift_right_logical(lane + base, 5) & 31
        ends = {1: along_x >= 1, -1: along_x <= 30}
        sides = {1: along_y >= 1, -1: along_y <= 30}
        margin = jnp.zeros((8, EDGE), F32)
        by_plane = {}
        for a in (-1, 0, 1):
            total = None
            for b in (-1, 0, 1):
                line = None
                for c in (-1, 0, 1):
                    index = 9 * (a + 1) + 3 * (b + 1) + (c + 1)
                    term = terms[pl.ds(pl.multiple_of(index * GROUP + group * 8, 8), 8), :]
                    if c != 0:
                        term = shift(jnp.where(ends[sign * c], term, 0.0), sign * c)
                    line = term if line is None else line + term
                if b != 0:
                    line = jnp.where(sides[sign * b], line, 0.0)
                line = jnp.concatenate([margin, line, margin], axis=1)
                if b != 0:
                    line = shift(line, sign * b * 32)
                total = line if total is None else total + line
            by_plane[sign * a] = total
        low, mid, high = by_plane[1], by_plane[0], by_plane[-1]
        pieces = (
            (0, low[:, :1024]),
            (1024, low[:, 1024:] + mid[:, :768]),
            (1792, mid[:, 768:1024]),
            (2048, mid[:, 1024:] + high[:, :768]),
            (2816, high[:, 768:]),
        )
        for start, piece in pieces:
            stop = start + piece.shape[1]
            out_ref[2 * group, :, start:stop] = piece[:OWN].astype(out_ref.dtype)
            out_ref[2 * group + 1, :, start:stop] = piece[OWN:].astype(out_ref.dtype)
        return carry

    lax.fori_loop(0, GROUP // 8, rows, 0)


def forward_kernel(low_ref, high_ref, lower_ref, upper_ref, out_ref, sums_ref, terms, held):
    at = pl.program_id(0)

    @pl.when(at == 0)
    def _():
        held[...] = jnp.zeros_like(held)

    def columns(step, carry):
        part = pl.ds(pl.multiple_of(step * 256, 256), 256)
        terms[:, part] = nt_dot(low_ref[...], lower_ref[part, :]) + nt_dot(
            high_ref[...], upper_ref[part, :]
        )
        return carry

    lax.fori_loop(0, PLANE // 256, columns, 0)
    lane = iota((8, PLANE), 1)
    along_x, along_y = lane & 31, lax.shift_right_logical(lane, 5)
    ends = {1: along_x >= 1, -1: along_x <= 30}
    sides = {1: along_y >= 1, -1: along_y <= 30}
    for a in (-1, 0, 1):
        total = None
        for b in (-1, 0, 1):
            line = None
            for c in (-1, 0, 1):
                index = 9 * (a + 1) + 3 * (b + 1) + (c + 1)
                term = terms[8 * index : 8 * index + 8, :]
                if c != 0:
                    term = shift(jnp.where(ends[c], term, 0.0), c)
                line = term if line is None else line + term
            if b != 0:
                line = shift(jnp.where(sides[b], line, 0.0), 32 * b)
            total = line if total is None else total + line
        goal = pl.ds(pl.multiple_of((at + 1 - a) * PLANE, PLANE), PLANE)
        held[:, goal] += total

    @pl.when(at == HALF - 1)
    def _():
        total = jnp.zeros((OWN, 128), F32)
        squares = jnp.zeros((OWN, 128), F32)
        for z in range(2 * HALF):
            side, own = divmod(z, HALF)
            cells = held[OWN * side : OWN * side + OWN, (own + 1) * PLANE : (own + 2) * PLANE]
            if z == HALF - 1:
                cells = cells + held[OWN:, :PLANE]
            if z == HALF:
                cells = cells + held[:OWN, (HALF + 1) * PLANE :]
            out_ref[:, z * PLANE : (z + 1) * PLANE] = cells
            total = total + lane_sum(cells)
            squares = squares + lane_sum(cells * cells)
        row = in_lanes([total, squares])
        for vol in range(sums_ref.shape[0]):
            sums_ref[vol] = row


def backward_kernel(base_ref, weight_ref, grads_ref, out_ref, terms):
    def columns(step, carry):
        part = pl.ds(pl.multiple_of(step * 256, 256), 256)
        terms[:, part] = jnp.dot(
            weight_ref[...], grads_ref[:, part], preferred_element_type=F32
        )
        return carry

    lax.fori_loop(0, BLOCK // 256, columns, 0)
    spread(base_ref[0], terms, out_ref, -1)


def filter_kernel(base_ref, grads_ref, acts_ref, out_ref, copies, product):
    base = base_ref[0]

    def rows(group, carry):
        lane = iota((16, SPAN), 1)
        along_x = lane & 31
        along_y = lax.shift_right_logical(lane + (base + 2 * PLANE - REACH), 5) & 31
        first = pl.multiple_of(group * 16, 16)
        acts = acts_ref[pl.ds(first, 16), :].astype(F32)
        ends = {1: along_x <= 30, -1: along_x >= 1}
        sides = {1: along_y <= 30, -1: along_y >= 1}
        for b in (-1, 0, 1):
            for c in (-1, 0, 1):
                moved = acts
                if b != 0 or c != 0:
                    moved = shift(acts, 32 * b + c)
                if c != 0:
                    moved = jnp.where(ends[c], moved, 0.0)
                if b != 0:
                    moved = jnp.where(sides[b], moved, 0.0)
                moved = moved.astype(BF16)
                for a in (-1, 0, 1):
                    index = 9 * (a + 1) + 3 * (b + 1) + (c + 1)
                    start = REACH + PLANE * a
                    copies[pl.ds(index * GROUP + first, 16), :] = moved[:, start : start + BLOCK]
        return carry

    lax.fori_loop(0, GROUP // 16, rows, 0)
    copies[ROWS:, :] = jnp.zeros((1024 - ROWS, BLOCK), BF16)

    def offsets(step, carry):
        part = pl.ds(pl.multiple_of(step * 256, 256), 256)
        product[:, part] = nt_dot(grads_ref[...], copies[part, :]).astype(BF16)
        return carry

    lax.fori_loop(0, 4, offsets, 0)

    def owners(step, carry):
        of = iota((1024, 256), 0)
        to = iota((1024, 256), 1)
        same = (
            (2 * step + lax.shift_right_logical(to, 7)) == (lax.shift_right_logical(of, 2) & 7)
        ) & ((to & 127) == (lax.shift_right_logical(of, 5) * 4 + (of & 3)))
        select = jnp.where(same, 1.0, 0.0).astype(BF16)
        placed = jnp.dot(product[...], select, preferred_element_type=F32).astype(BF16)
        for vol in range(8):
            for half in range(2):
                out_ref[vol, 2 * step + half] = placed[
                    32 * vol : 32 * vol + 32, 128 * half : 128 * half + 128
                ]
        return carry

    lax.fori_loop(0, 4, owners, 0)


def lane_sum(value):
    parts = value[:, :128]
    for start in range(128, value.shape[1], 128):
        parts = parts + value[:, start : start + 128]
    return jnp.broadcast_to(jnp.sum(parts, axis=1, keepdims=True), (value.shape[0], 128))


def in_lanes(values):
    lane = iota((OWN, 128), 1)
    row = jnp.zeros((OWN, 128), F32)
    for index, value in enumerate(values):
        row = jnp.where(lane == index, value, row)
    return row


def from_lanes(total, count):
    lane = iota((OWN, 128), 1)
    return [
        jnp.sum(jnp.where(lane == index, total, 0.0), axis=1, keepdims=True)
        for index in range(count)
    ]


def sums_kernel(saved_ref, upstream_ref, sums_ref):
    saved = saved_ref[...].astype(F32)
    upstream = upstream_ref[...].astype(F32)
    sums_ref[...] = in_lanes(
        [
            lane_sum(saved),
            lane_sum(saved * saved),
            lane_sum(upstream),
            lane_sum(upstream * saved),
        ]
    )


def pack_kernel(acts_ref, packed_ref):
    for block in range(NY):
        start = block * BLOCK - REACH
        low, high = max(start, 0), min(start + SPAN, CELLS)
        packed_ref[block, :, low - start : high - start] = acts_ref[:, low:high]
        if low > start:
            packed_ref[block, :, : low - start] = jnp.zeros((OWN, low - start), BF16)
        if high < start + SPAN:
            packed_ref[block, :, high - start :] = jnp.zeros((OWN, start + SPAN - high), BF16)


def grad_kernel(counted, saved_ref, upstream_ref, sums_ref, params_ref, packed_ref, means_ref):
    saved_sum, square_sum, upstream_sum, product_sum = from_lanes(sums_ref[...], 4)
    mean = saved_sum / counted
    var = square_sum / counted - mean * mean
    inverse = lax.rsqrt(var + EPSILON)
    shift_grad = upstream_sum / counted
    gain_grad = (product_sum / counted - mean * shift_grad) * inverse
    means_ref[...] = in_lanes([gain_grad, shift_grad])
    scale = params_ref[2][:, :1] * inverse
    for block in range(NY):
        part = slice(block * BLOCK, (block + 1) * BLOCK)
        normed = (saved_ref[:, part].astype(F32) - mean) * inverse
        upstream = upstream_ref[:, part].astype(F32)
        grads = (scale * (upstream - shift_grad - normed * gain_grad)).astype(BF16)
        for to in range(NZ):
            packed_ref[block * NZ + to] = grads


def joined(parts_ref, block):
    whole = parts_ref[block, :, REACH : REACH + BLOCK].astype(F32)
    pieces = [whole[:, :384], whole[:, 384:REACH], whole[:, REACH:]]
    if block > 0:
        before = parts_ref[block - 1, :, REACH + BLOCK :].astype(F32)
        pieces[0] = pieces[0] + before[:, :384]
        pieces[1] = pieces[1] + before[:, 384:]
    if block < NY - 1:
        after = parts_ref[block + 1, :, :REACH].astype(F32)
        pieces[1] = pieces[1] + after[:, : REACH - 384]
        pieces[2] = pieces[2] + after[:, REACH - 384 :]
    return jnp.concatenate(pieces, axis=1)


def join_kernel(parts_ref, out_ref):
    for block in range(NY):
        out_ref[:, block * BLOCK : (block + 1) * BLOCK] = joined(parts_ref, block).astype(BF16)


def relu_kernel(counted, conv_ref, sums_ref, params_ref, out_ref):
    total = sums_ref[0]
    for vol in range(1, sums_ref.shape[0]):
        total = total + sums_ref[vol]
    first_sum, square_sum = from_lanes(total, 2)
    mean = first_sum / counted
    var = square_sum / counted - mean * mean
    scale = params_ref[0][:, :1] * lax.rsqrt(var + EPSILON)
    bias = params_ref[1][:, :1]
    out_ref[...] = jnp.maximum((conv_ref[...] - mean) * scale + bias, 0.0).astype(BF16)


def shaped(shape, dtype):
    return jax.ShapeDtypeStruct(shape, dtype)


def call(kernel, outs, specs, scratch=()):
    return pl.pallas_call(
        kernel,
        out_shape=outs,
        in_specs=specs,
        out_specs=jax.tree.map(lambda _: VMEM, outs),
        scratch_shapes=list(scratch),
        compiler_params=PARAMS,
        cost_estimate=pl.CostEstimate(flops=1000, bytes_accessed=1000, transcendentals=0),
    )


def exchange(value, axes):
    return lax.all_to_all(value, axes, 0, 0, tiled=True)


def gathered(filters):
    filters = lax.all_gather(filters, "y", axis=0, tiled=False)
    return jnp.transpose(filters, (1, 0, 2, 3)).reshape(ROWS, CH)


def shards(
    fwd_input,
    weight_one,
    gain_one,
    bias_one,
    saved_conv,
    cotangent,
    saved_input,
    weight_two,
    gain_two,
):
    volumes = lax.axis_size("vol")
    counted = volumes * CELLS
    base = (lax.axis_index("y") * BLOCK).astype(jnp.int32).reshape(1)
    params = jnp.broadcast_to(
        jnp.stack([gain_one, bias_one, gain_two])[:, :, None], (3, OWN, 128)
    )
    saved, upstream = saved_conv[0], cotangent[0]

    cells = lax.all_gather(fwd_input[0].T, ("y", "z"), axis=0, tiled=True)
    low = jnp.pad(weight_one, ((0, 0), (0, OWN), (0, 0))).reshape(27 * 2 * OWN, CH)
    high = jnp.pad(weight_one, ((0, 0), (OWN, 0), (0, 0))).reshape(27 * 2 * OWN, CH)

    sums_two = call(sums_kernel, shaped((OWN, 128), F32), [VMEM] * 2)(saved, upstream)
    acts = call(pack_kernel, shaped((NY, OWN, SPAN), BF16), [VMEM])(saved_input[0])
    acts = exchange(acts, "y")
    sums_two = lax.psum(sums_two, "vol")
    acts, sums_two = lax.optimization_barrier((acts, sums_two))
    acts = acts.reshape(GROUP, SPAN)
    packed, means = call(
        lambda *refs: grad_kernel(counted, *refs),
        (shaped((NY * NZ, OWN, BLOCK), BF16), shaped((OWN, 128), F32)),
        [VMEM] * 4,
    )(saved, upstream, sums_two, params)

    second, packed = lax.optimization_barrier((weight_two, packed))
    grads = exchange(packed, ("y", "z"))
    second = gathered(jnp.transpose(second, (0, 2, 1)))
    grads, second = lax.optimization_barrier((grads, second))
    grads = grads.reshape(CH, BLOCK)
    filter_parts = call(
        filter_kernel,
        shaped((8, NY, GROUP, 128), BF16),
        [SMEM, VMEM, VMEM],
        [pltpu.VMEM((1024, BLOCK), BF16), pltpu.VMEM((CH, 1024), BF16)],
    )(base, grads, acts)
    second, filter_parts = lax.optimization_barrier((second, filter_parts))
    filter_parts = exchange(filter_parts.reshape(8 * NY, GROUP, 128), ("vol", "y"))
    input_parts = call(
        backward_kernel,
        shaped((NY, OWN, SPAN), BF16),
        [SMEM, VMEM, VMEM],
        [pltpu.VMEM((ROWS, BLOCK), F32)],
    )(base, second, grads)

    after = input_parts, filter_parts
    cells, after = lax.optimization_barrier((cells, after))
    input_parts = exchange(input_parts, "y")
    conv_out, sums_one = pl.pallas_call(
        forward_kernel,
        out_shape=(shaped((OWN, CELLS), F32), shaped((volumes, OWN, 128), F32)),
        grid=(HALF,),
        in_specs=[
            pl.BlockSpec((27 * 2 * OWN, CH), lambda at: (0, 0)),
            pl.BlockSpec((27 * 2 * OWN, CH), lambda at: (0, 0)),
            pl.BlockSpec((PLANE, CH), lambda at: (at, 0)),
            pl.BlockSpec((PLANE, CH), lambda at: (at + HALF, 0)),
        ],
        out_specs=(
            pl.BlockSpec((OWN, CELLS), lambda at: (0, 0)),
            pl.BlockSpec((volumes, OWN, 128), lambda at: (0, 0, 0)),
        ),
        scratch_shapes=[
            pltpu.VMEM((27 * 2 * OWN, PLANE), F32),
            pltpu.VMEM((2 * OWN, (HALF + 2) * PLANE), F32),
        ],
        compiler_params=pltpu.CompilerParams(vmem_limit_bytes=58 * 1024 * 1024),
        cost_estimate=pl.CostEstimate(flops=1000, bytes_accessed=1000, transcendentals=0),
    )(low, high, cells, cells)
    sums_one = exchange(sums_one, "vol")
    activation = call(
        lambda *refs: relu_kernel(counted, *refs), shaped((OWN, CELLS), BF16), [VMEM] * 3
    )(conv_out, sums_one, params)
    input_grad = call(join_kernel, shaped((OWN, CELLS), BF16), [VMEM])(input_parts)

    summed = jnp.sum(filter_parts.astype(F32), axis=0) / math.sqrt(counted)
    weight_grad = jnp.transpose(summed[:, : 27 * OWN].reshape(GROUP, 27, OWN), (1, 0, 2))
    return (activation[None], input_grad[None], weight_grad, means[:, 0], means[:, 1])


def solution(mesh):
    cut = Mesh(mesh.devices.reshape(mesh.devices.shape[0], NY, NZ), ("vol", "y", "z"))
    chan = ("y", "z")
    return jax.shard_map(
        shards,
        mesh=cut,
        in_specs=(
            P("vol", None, chan),
            P(None, chan, None),
            P(chan),
            P(chan),
            P("vol", chan, None),
            P("vol", chan, None),
            P("vol", chan, None),
            P(None, None, chan),
            P(chan),
        ),
        out_specs=(
            P("vol", chan, None),
            P("vol", chan, None),
            P(None, "vol", chan),
            P(chan),
            P(chan),
        ),
        check_vma=False,
    )
```

```python
import math

import jax
import jax.numpy as jnp
from jax import lax
from jax.experimental import pallas as pl
from jax.experimental.pallas import tpu as pltpu
from jax.sharding import Mesh
from jax.sharding import PartitionSpec as P

PLANE = 1024
BLOCK = 1536
EDGE = 128
REACH = PLANE + EDGE
SPAN = BLOCK + 2 * REACH
CELLS = 12288
HALF = 6
NY = 8
NZ = 8
OWN = 4
GROUP = NY * OWN
CH = 256
ROWS = 27 * GROUP
EPSILON = 1e-05
F32 = jnp.float32
BF16 = jnp.bfloat16

VMEM = pl.BlockSpec(memory_space=pltpu.VMEM)
SMEM = pl.BlockSpec(memory_space=pltpu.SMEM)
PARAMS = pltpu.CompilerParams(vmem_limit_bytes=40 * 1024 * 1024)


def iota(shape, axis):
    return lax.broadcasted_iota(jnp.int32, shape, axis)


def shift(value, amount):
    lanes = value.shape[1]
    return pltpu.roll(value, (-amount) % lanes, 1)


def nt_dot(left, right):
    return lax.dot_general(left, right, (((1,), (1,)), ((), ())), preferred_element_type=F32)


def spread(base, terms, out_ref, sign):
    def rows(group, carry):
        lane = iota((8, BLOCK), 1)
        along_x = lane & 31
        along_y = lax.shift_right_logical(lane + base, 5) & 31
        ends = {1: along_x >= 1, -1: along_x <= 30}
        sides = {1: along_y >= 1, -1: along_y <= 30}
        margin = jnp.zeros((8, EDGE), F32)
        by_plane = {}
        for a in (-1, 0, 1):
            total = None
            for b in (-1, 0, 1):
                line = None
                for c in (-1, 0, 1):
                    index = 9 * (a + 1) + 3 * (b + 1) + (c + 1)
                    term = terms[pl.ds(pl.multiple_of(index * GROUP + group * 8, 8), 8), :]
                    if c != 0:
                        term = shift(jnp.where(ends[sign * c], term, 0.0), sign * c)
                    line = term if line is None else line + term
                if b != 0:
                    line = jnp.where(sides[sign * b], line, 0.0)
                line = jnp.concatenate([margin, line, margin], axis=1)
                if b != 0:
                    line = shift(line, sign * b * 32)
                total = line if total is None else total + line
            by_plane[sign * a] = total
        low, mid, high = by_plane[1], by_plane[0], by_plane[-1]
        pieces = (
            (0, low[:, :1024]),
            (1024, low[:, 1024:] + mid[:, :768]),
            (1792, mid[:, 768:1024]),
            (2048, mid[:, 1024:] + high[:, :768]),
            (2816, high[:, 768:]),
        )
        for start, piece in pieces:
            stop = start + piece.shape[1]
            out_ref[2 * group, :, start:stop] = piece[:OWN].astype(out_ref.dtype)
            out_ref[2 * group + 1, :, start:stop] = piece[OWN:].astype(out_ref.dtype)
        return carry

    lax.fori_loop(0, GROUP // 8, rows, 0)


def forward_kernel(low_ref, high_ref, lower_ref, upper_ref, out_ref, sums_ref, terms, held):
    at = pl.program_id(0)

    @pl.when(at == 0)
    def _():
        held[...] = jnp.zeros_like(held)

    def columns(step, carry):
        part = pl.ds(pl.multiple_of(step * 256, 256), 256)
        terms[:, part] = nt_dot(low_ref[...], lower_ref[part, :]) + nt_dot(
            high_ref[...], upper_ref[part, :]
        )
        return carry

    lax.fori_loop(0, PLANE // 256, columns, 0)
    lane = iota((8, PLANE), 1)
    along_x, along_y = lane & 31, lax.shift_right_logical(lane, 5)
    ends = {1: along_x >= 1, -1: along_x <= 30}
    sides = {1: along_y >= 1, -1: along_y <= 30}
    for a in (-1, 0, 1):
        total = None
        for b in (-1, 0, 1):
            line = None
            for c in (-1, 0, 1):
                index = 9 * (a + 1) + 3 * (b + 1) + (c + 1)
                term = terms[8 * index : 8 * index + 8, :]
                if c != 0:
                    term = shift(jnp.where(ends[c], term, 0.0), c)
                line = term if line is None else line + term
            if b != 0:
                line = shift(jnp.where(sides[b], line, 0.0), 32 * b)
            total = line if total is None else total + line
        goal = pl.ds(pl.multiple_of((at + 1 - a) * PLANE, PLANE), PLANE)
        held[:, goal] += total

    @pl.when(at == HALF - 1)
    def _():
        total = jnp.zeros((OWN, 128), F32)
        squares = jnp.zeros((OWN, 128), F32)
        for z in range(2 * HALF):
            side, own = divmod(z, HALF)
            cells = held[OWN * side : OWN * side + OWN, (own + 1) * PLANE : (own + 2) * PLANE]
            if z == HALF - 1:
                cells = cells + held[OWN:, :PLANE]
            if z == HALF:
                cells = cells + held[:OWN, (HALF + 1) * PLANE :]
            out_ref[:, z * PLANE : (z + 1) * PLANE] = cells
            total = total + lane_sum(cells)
            squares = squares + lane_sum(cells * cells)
        row = in_lanes([total, squares])
        for vol in range(sums_ref.shape[0]):
            sums_ref[vol] = row


def backward_kernel(base_ref, weight_ref, grads_ref, out_ref, terms):
    def columns(step, carry):
        part = pl.ds(pl.multiple_of(step * 256, 256), 256)
        terms[:, part] = jnp.dot(
            weight_ref[...], grads_ref[:, part], preferred_element_type=F32
        )
        return carry

    lax.fori_loop(0, BLOCK // 256, columns, 0)
    spread(base_ref[0], terms, out_ref, -1)


def filter_kernel(base_ref, grads_ref, acts_ref, out_ref, copies, product):
    base = base_ref[0]

    def rows(group, carry):
        lane = iota((16, SPAN), 1)
        along_x = lane & 31
        along_y = lax.shift_right_logical(lane + (base + 2 * PLANE - REACH), 5) & 31
        first = pl.multiple_of(group * 16, 16)
        acts = acts_ref[pl.ds(first, 16), :].astype(F32)
        ends = {1: along_x <= 30, -1: along_x >= 1}
        sides = {1: along_y <= 30, -1: along_y >= 1}
        for b in (-1, 0, 1):
            for c in (-1, 0, 1):
                moved = acts
                if b != 0 or c != 0:
                    moved = shift(acts, 32 * b + c)
                if c != 0:
                    moved = jnp.where(ends[c], moved, 0.0)
                if b != 0:
                    moved = jnp.where(sides[b], moved, 0.0)
                moved = moved.astype(BF16)
                for a in (-1, 0, 1):
                    index = 9 * (a + 1) + 3 * (b + 1) + (c + 1)
                    start = REACH + PLANE * a
                    copies[pl.ds(index * GROUP + first, 16), :] = moved[:, start : start + BLOCK]
        return carry

    lax.fori_loop(0, GROUP // 16, rows, 0)
    copies[ROWS:, :] = jnp.zeros((1024 - ROWS, BLOCK), BF16)

    def offsets(step, carry):
        part = pl.ds(pl.multiple_of(step * 256, 256), 256)
        product[:, part] = nt_dot(grads_ref[...], copies[part, :]).astype(BF16)
        return carry

    lax.fori_loop(0, 4, offsets, 0)

    def owners(step, carry):
        of = iota((1024, 256), 0)
        to = iota((1024, 256), 1)
        same = (
            (2 * step + lax.shift_right_logical(to, 7)) == (lax.shift_right_logical(of, 2) & 7)
        ) & ((to & 127) == (lax.shift_right_logical(of, 5) * 4 + (of & 3)))
        select = jnp.where(same, 1.0, 0.0).astype(BF16)
        placed = jnp.dot(product[...], select, preferred_element_type=F32).astype(BF16)
        for vol in range(8):
            for half in range(2):
                out_ref[vol, 2 * step + half] = placed[
                    32 * vol : 32 * vol + 32, 128 * half : 128 * half + 128
                ]
        return carry

    lax.fori_loop(0, 4, owners, 0)


def lane_sum(value):
    parts = value[:, :128]
    for start in range(128, value.shape[1], 128):
        parts = parts + value[:, start : start + 128]
    return jnp.broadcast_to(jnp.sum(parts, axis=1, keepdims=True), (value.shape[0], 128))


def in_lanes(values):
    lane = iota((OWN, 128), 1)
    row = jnp.zeros((OWN, 128), F32)
    for index, value in enumerate(values):
        row = jnp.where(lane == index, value, row)
    return row


def from_lanes(total, count):
    lane = iota((OWN, 128), 1)
    return [
        jnp.sum(jnp.where(lane == index, total, 0.0), axis=1, keepdims=True)
        for index in range(count)
    ]


def sums_kernel(saved_ref, upstream_ref, sums_ref):
    saved = saved_ref[...].astype(F32)
    upstream = upstream_ref[...].astype(F32)
    sums_ref[...] = in_lanes(
        [
            lane_sum(saved),
            lane_sum(saved * saved),
            lane_sum(upstream),
            lane_sum(upstream * saved),
        ]
    )


def pack_kernel(acts_ref, packed_ref):
    for block in range(NY):
        start = block * BLOCK - REACH
        low, high = max(start, 0), min(start + SPAN, CELLS)
        packed_ref[block, :, low - start : high - start] = acts_ref[:, low:high]
        if low > start:
            packed_ref[block, :, : low - start] = jnp.zeros((OWN, low - start), BF16)
        if high < start + SPAN:
            packed_ref[block, :, high - start :] = jnp.zeros((OWN, start + SPAN - high), BF16)


def grad_kernel(counted, saved_ref, upstream_ref, sums_ref, params_ref, packed_ref, means_ref):
    saved_sum, square_sum, upstream_sum, product_sum = from_lanes(sums_ref[...], 4)
    mean = saved_sum / counted
    var = square_sum / counted - mean * mean
    inverse = lax.rsqrt(var + EPSILON)
    shift_grad = upstream_sum / counted
    gain_grad = (product_sum / counted - mean * shift_grad) * inverse
    means_ref[...] = in_lanes([gain_grad, shift_grad])
    scale = params_ref[2][:, :1] * inverse
    for block in range(NY):
        part = slice(block * BLOCK, (block + 1) * BLOCK)
        normed = (saved_ref[:, part].astype(F32) - mean) * inverse
        upstream = upstream_ref[:, part].astype(F32)
        grads = (scale * (upstream - shift_grad - normed * gain_grad)).astype(BF16)
        for to in range(NZ):
            packed_ref[block * NZ + to] = grads


def joined(parts_ref, block):
    whole = parts_ref[block, :, REACH : REACH + BLOCK].astype(F32)
    pieces = [whole[:, :384], whole[:, 384:REACH], whole[:, REACH:]]
    if block > 0:
        before = parts_ref[block - 1, :, REACH + BLOCK :].astype(F32)
        pieces[0] = pieces[0] + before[:, :384]
        pieces[1] = pieces[1] + before[:, 384:]
    if block < NY - 1:
        after = parts_ref[block + 1, :, :REACH].astype(F32)
        pieces[1] = pieces[1] + after[:, : REACH - 384]
        pieces[2] = pieces[2] + after[:, REACH - 384 :]
    return jnp.concatenate(pieces, axis=1)


def join_kernel(parts_ref, out_ref):
    for block in range(NY):
        out_ref[:, block * BLOCK : (block + 1) * BLOCK] = joined(parts_ref, block).astype(BF16)


def relu_kernel(counted, conv_ref, sums_ref, params_ref, out_ref):
    total = sums_ref[0]
    for vol in range(1, sums_ref.shape[0]):
        total = total + sums_ref[vol]
    first_sum, square_sum = from_lanes(total, 2)
    mean = first_sum / counted
    var = square_sum / counted - mean * mean
    scale = params_ref[0][:, :1] * lax.rsqrt(var + EPSILON)
    bias = params_ref[1][:, :1]
    out_ref[...] = jnp.maximum((conv_ref[...] - mean) * scale + bias, 0.0).astype(BF16)


def shaped(shape, dtype):
    return jax.ShapeDtypeStruct(shape, dtype)


def call(kernel, outs, specs, scratch=()):
    return pl.pallas_call(
        kernel,
        out_shape=outs,
        in_specs=specs,
        out_specs=jax.tree.map(lambda _: VMEM, outs),
        scratch_shapes=list(scratch),
        compiler_params=PARAMS,
        cost_estimate=pl.CostEstimate(flops=1000, bytes_accessed=1000, transcendentals=0),
    )


def exchange(value, axes):
    return lax.all_to_all(value, axes, 0, 0, tiled=True)


def gathered(filters):
    filters = lax.all_gather(filters, "y", axis=0, tiled=False)
    return jnp.transpose(filters, (1, 0, 2, 3)).reshape(ROWS, CH)


def shards(
    fwd_input,
    weight_one,
    gain_one,
    bias_one,
    saved_conv,
    cotangent,
    saved_input,
    weight_two,
    gain_two,
):
    volumes = lax.axis_size("vol")
    counted = volumes * CELLS
    base = (lax.axis_index("y") * BLOCK).astype(jnp.int32).reshape(1)
    params = jnp.broadcast_to(
        jnp.stack([gain_one, bias_one, gain_two])[:, :, None], (3, OWN, 128)
    )
    saved, upstream = saved_conv[0], cotangent[0]

    cells = lax.all_gather(fwd_input[0].T, ("y", "z"), axis=0, tiled=True)
    low = jnp.pad(weight_one, ((0, 0), (0, OWN), (0, 0))).reshape(27 * 2 * OWN, CH)
    high = jnp.pad(weight_one, ((0, 0), (OWN, 0), (0, 0))).reshape(27 * 2 * OWN, CH)

    sums_two = call(sums_kernel, shaped((OWN, 128), F32), [VMEM] * 2)(saved, upstream)
    acts = call(pack_kernel, shaped((NY, OWN, SPAN), BF16), [VMEM])(saved_input[0])
    acts = exchange(acts, "y")
    sums_two = lax.psum(sums_two, "vol")
    acts, sums_two = lax.optimization_barrier((acts, sums_two))
    acts = acts.reshape(GROUP, SPAN)
    packed, means = call(
        lambda *refs: grad_kernel(counted, *refs),
        (shaped((NY * NZ, OWN, BLOCK), BF16), shaped((OWN, 128), F32)),
        [VMEM] * 4,
    )(saved, upstream, sums_two, params)

    second, packed = lax.optimization_barrier((weight_two, packed))
    grads = exchange(packed, ("y", "z"))
    second = gathered(jnp.transpose(second, (0, 2, 1)))
    grads, second = lax.optimization_barrier((grads, second))
    grads = grads.reshape(CH, BLOCK)
    filter_parts = call(
        filter_kernel,
        shaped((8, NY, GROUP, 128), BF16),
        [SMEM, VMEM, VMEM],
        [pltpu.VMEM((1024, BLOCK), BF16), pltpu.VMEM((CH, 1024), BF16)],
    )(base, grads, acts)
    second, filter_parts = lax.optimization_barrier((second, filter_parts))
    input_parts = call(
        backward_kernel,
        shaped((NY, OWN, SPAN), BF16),
        [SMEM, VMEM, VMEM],
        [pltpu.VMEM((ROWS, BLOCK), F32)],
    )(base, second, grads)

    input_parts = exchange(input_parts, "y")

    filter_parts, _ = lax.optimization_barrier((filter_parts, input_parts))
    filter_parts = exchange(filter_parts.reshape(8 * NY, GROUP, 128), ("vol", "y"))
    cells, _ = lax.optimization_barrier((cells, input_parts))
    conv_out, sums_one = pl.pallas_call(
        forward_kernel,
        out_shape=(shaped((OWN, CELLS), F32), shaped((volumes, OWN, 128), F32)),
        grid=(HALF,),
        in_specs=[
            pl.BlockSpec((27 * 2 * OWN, CH), lambda at: (0, 0)),
            pl.BlockSpec((27 * 2 * OWN, CH), lambda at: (0, 0)),
            pl.BlockSpec((PLANE, CH), lambda at: (at, 0)),
            pl.BlockSpec((PLANE, CH), lambda at: (at + HALF, 0)),
        ],
        out_specs=(
            pl.BlockSpec((OWN, CELLS), lambda at: (0, 0)),
            pl.BlockSpec((volumes, OWN, 128), lambda at: (0, 0, 0)),
        ),
        scratch_shapes=[
            pltpu.VMEM((27 * 2 * OWN, PLANE), F32),
            pltpu.VMEM((2 * OWN, (HALF + 2) * PLANE), F32),
        ],
        compiler_params=pltpu.CompilerParams(vmem_limit_bytes=58 * 1024 * 1024),
        cost_estimate=pl.CostEstimate(flops=1000, bytes_accessed=1000, transcendentals=0),
    )(low, high, cells, cells)
    sums_one = exchange(sums_one, "vol")
    activation = call(
        lambda *refs: relu_kernel(counted, *refs), shaped((OWN, CELLS), BF16), [VMEM] * 3
    )(conv_out, sums_one, params)
    input_grad = call(join_kernel, shaped((OWN, CELLS), BF16), [VMEM])(input_parts)

    summed = jnp.sum(filter_parts.astype(F32), axis=0) / math.sqrt(counted)
    weight_grad = jnp.transpose(summed[:, : 27 * OWN].reshape(GROUP, 27, OWN), (1, 0, 2))
    return (activation[None], input_grad[None], weight_grad, means[:, 0], means[:, 1])


def solution(mesh):
    cut = Mesh(mesh.devices.reshape(mesh.devices.shape[0], NY, NZ), ("vol", "y", "z"))
    chan = ("y", "z")
    return jax.shard_map(
        shards,
        mesh=cut,
        in_specs=(
            P("vol", None, chan),
            P(None, chan, None),
            P(chan),
            P(chan),
            P("vol", chan, None),
            P("vol", chan, None),
            P("vol", chan, None),
            P(None, None, chan),
            P(chan),
        ),
        out_specs=(
            P("vol", chan, None),
            P("vol", chan, None),
            P(None, "vol", chan),
            P(chan),
            P(chan),
        ),
        check_vma=False,
    )
```

```python
import math

import jax
import jax.numpy as jnp
from jax import lax
from jax.experimental import pallas as pl
from jax.experimental.pallas import tpu as pltpu
from jax.sharding import Mesh
from jax.sharding import PartitionSpec as P

PLANE = 1024
BLOCK = 1536
EDGE = 128
REACH = PLANE + EDGE
SPAN = BLOCK + 2 * REACH
CELLS = 12288
HALF = 6
NY = 8
NZ = 8
OWN = 4
GROUP = NY * OWN
CH = 256
ROWS = 27 * GROUP
EPSILON = 1e-05
F32 = jnp.float32
BF16 = jnp.bfloat16

VMEM = pl.BlockSpec(memory_space=pltpu.VMEM)
SMEM = pl.BlockSpec(memory_space=pltpu.SMEM)
PARAMS = pltpu.CompilerParams(vmem_limit_bytes=40 * 1024 * 1024)


def iota(shape, axis):
    return lax.broadcasted_iota(jnp.int32, shape, axis)


def shift(value, amount):
    lanes = value.shape[1]
    return pltpu.roll(value, (-amount) % lanes, 1)


def nt_dot(left, right):
    return lax.dot_general(left, right, (((1,), (1,)), ((), ())), preferred_element_type=F32)


def spread(base, terms, out_ref, sign):
    def rows(group, carry):
        lane = iota((8, BLOCK), 1)
        along_x = lane & 31
        along_y = lax.shift_right_logical(lane + base, 5) & 31
        ends = {1: along_x >= 1, -1: along_x <= 30}
        sides = {1: along_y >= 1, -1: along_y <= 30}
        margin = jnp.zeros((8, EDGE), F32)
        by_plane = {}
        for a in (-1, 0, 1):
            total = None
            for b in (-1, 0, 1):
                line = None
                for c in (-1, 0, 1):
                    index = 9 * (a + 1) + 3 * (b + 1) + (c + 1)
                    term = terms[pl.ds(pl.multiple_of(index * GROUP + group * 8, 8), 8), :]
                    if c != 0:
                        term = shift(jnp.where(ends[sign * c], term, 0.0), sign * c)
                    line = term if line is None else line + term
                if b != 0:
                    line = jnp.where(sides[sign * b], line, 0.0)
                line = jnp.concatenate([margin, line, margin], axis=1)
                if b != 0:
                    line = shift(line, sign * b * 32)
                total = line if total is None else total + line
            by_plane[sign * a] = total
        low, mid, high = by_plane[1], by_plane[0], by_plane[-1]
        pieces = (
            (0, low[:, :1024]),
            (1024, low[:, 1024:] + mid[:, :768]),
            (1792, mid[:, 768:1024]),
            (2048, mid[:, 1024:] + high[:, :768]),
            (2816, high[:, 768:]),
        )
        for start, piece in pieces:
            stop = start + piece.shape[1]
            out_ref[2 * group, :, start:stop] = piece[:OWN].astype(out_ref.dtype)
            out_ref[2 * group + 1, :, start:stop] = piece[OWN:].astype(out_ref.dtype)
        return carry

    lax.fori_loop(0, GROUP // 8, rows, 0)


def forward_kernel(low_ref, high_ref, lower_ref, upper_ref, out_ref, sums_ref, terms, held):
    at = pl.program_id(0)

    @pl.when(at == 0)
    def _():
        held[...] = jnp.zeros_like(held)

    def columns(step, carry):
        part = pl.ds(pl.multiple_of(step * 256, 256), 256)
        terms[:, part] = nt_dot(low_ref[...], lower_ref[part, :]) + nt_dot(
            high_ref[...], upper_ref[part, :]
        )
        return carry

    lax.fori_loop(0, PLANE // 256, columns, 0)
    lane = iota((8, PLANE), 1)
    along_x, along_y = lane & 31, lax.shift_right_logical(lane, 5)
    ends = {1: along_x >= 1, -1: along_x <= 30}
    sides = {1: along_y >= 1, -1: along_y <= 30}
    for a in (-1, 0, 1):
        total = None
        for b in (-1, 0, 1):
            line = None
            for c in (-1, 0, 1):
                index = 9 * (a + 1) + 3 * (b + 1) + (c + 1)
                term = terms[8 * index : 8 * index + 8, :]
                if c != 0:
                    term = shift(jnp.where(ends[c], term, 0.0), c)
                line = term if line is None else line + term
            if b != 0:
                line = shift(jnp.where(sides[b], line, 0.0), 32 * b)
            total = line if total is None else total + line
        goal = pl.ds(pl.multiple_of((at + 1 - a) * PLANE, PLANE), PLANE)
        held[:, goal] += total

    @pl.when(at == HALF - 1)
    def _():
        total = jnp.zeros((OWN, 128), F32)
        squares = jnp.zeros((OWN, 128), F32)
        for z in range(2 * HALF):
            side, own = divmod(z, HALF)
            cells = held[OWN * side : OWN * side + OWN, (own + 1) * PLANE : (own + 2) * PLANE]
            if z == HALF - 1:
                cells = cells + held[OWN:, :PLANE]
            if z == HALF:
                cells = cells + held[:OWN, (HALF + 1) * PLANE :]
            out_ref[:, z * PLANE : (z + 1) * PLANE] = cells
            total = total + lane_sum(cells)
            squares = squares + lane_sum(cells * cells)
        sums_ref[...] = in_lanes([total, squares])


def backward_kernel(base_ref, weight_ref, grads_ref, out_ref, terms):
    def columns(step, carry):
        part = pl.ds(pl.multiple_of(step * 256, 256), 256)
        terms[:, part] = jnp.dot(
            weight_ref[...], grads_ref[:, part], preferred_element_type=F32
        )
        return carry

    lax.fori_loop(0, BLOCK // 256, columns, 0)
    spread(base_ref[0], terms, out_ref, -1)


def filter_kernel(base_ref, grads_ref, acts_ref, out_ref, copies, product):
    base = base_ref[0]

    def rows(group, carry):
        lane = iota((16, SPAN), 1)
        along_x = lane & 31
        along_y = lax.shift_right_logical(lane + (base + 2 * PLANE - REACH), 5) & 31
        first = pl.multiple_of(group * 16, 16)
        acts = acts_ref[pl.ds(first, 16), :].astype(F32)
        ends = {1: along_x <= 30, -1: along_x >= 1}
        sides = {1: along_y <= 30, -1: along_y >= 1}
        for b in (-1, 0, 1):
            for c in (-1, 0, 1):
                moved = acts
                if b != 0 or c != 0:
                    moved = shift(acts, 32 * b + c)
                if c != 0:
                    moved = jnp.where(ends[c], moved, 0.0)
                if b != 0:
                    moved = jnp.where(sides[b], moved, 0.0)
                moved = moved.astype(BF16)
                for a in (-1, 0, 1):
                    index = 9 * (a + 1) + 3 * (b + 1) + (c + 1)
                    start = REACH + PLANE * a
                    copies[pl.ds(index * GROUP + first, 16), :] = moved[:, start : start + BLOCK]
        return carry

    lax.fori_loop(0, GROUP // 16, rows, 0)
    copies[ROWS:, :] = jnp.zeros((1024 - ROWS, BLOCK), BF16)

    def offsets(step, carry):
        part = pl.ds(pl.multiple_of(step * 256, 256), 256)
        product[:, part] = nt_dot(grads_ref[...], copies[part, :]).astype(BF16)
        return carry

    lax.fori_loop(0, 4, offsets, 0)

    def owners(step, carry):
        of = iota((1024, 256), 0)
        to = iota((1024, 256), 1)
        same = (
            (2 * step + lax.shift_right_logical(to, 7)) == (lax.shift_right_logical(of, 2) & 7)
        ) & ((to & 127) == (lax.shift_right_logical(of, 5) * 4 + (of & 3)))
        select = jnp.where(same, 1.0, 0.0).astype(BF16)
        placed = jnp.dot(product[...], select, preferred_element_type=F32).astype(BF16)
        for vol in range(8):
            for half in range(2):
                out_ref[vol, 2 * step + half] = placed[
                    32 * vol : 32 * vol + 32, 128 * half : 128 * half + 128
                ]
        return carry

    lax.fori_loop(0, 4, owners, 0)


def lane_sum(value):
    parts = value[:, :128]
    for start in range(128, value.shape[1], 128):
        parts = parts + value[:, start : start + 128]
    return jnp.broadcast_to(jnp.sum(parts, axis=1, keepdims=True), (value.shape[0], 128))


def in_lanes(values):
    lane = iota((OWN, 128), 1)
    row = jnp.zeros((OWN, 128), F32)
    for index, value in enumerate(values):
        row = jnp.where(lane == index, value, row)
    return row


def from_lanes(sums_ref, count):
    total = sums_ref[...]
    lane = iota((OWN, 128), 1)
    return [
        jnp.sum(jnp.where(lane == index, total, 0.0), axis=1, keepdims=True)
        for index in range(count)
    ]


def sums_kernel(saved_ref, upstream_ref, sums_ref):
    saved = saved_ref[...].astype(F32)
    upstream = upstream_ref[...].astype(F32)
    sums_ref[...] = in_lanes(
        [
            lane_sum(saved),
            lane_sum(saved * saved),
            lane_sum(upstream),
            lane_sum(upstream * saved),
        ]
    )


def pack_kernel(acts_ref, packed_ref):
    for block in range(NY):
        start = block * BLOCK - REACH
        low, high = max(start, 0), min(start + SPAN, CELLS)
        packed_ref[block, :, low - start : high - start] = acts_ref[:, low:high]
        if low > start:
            packed_ref[block, :, : low - start] = jnp.zeros((OWN, low - start), BF16)
        if high < start + SPAN:
            packed_ref[block, :, high - start :] = jnp.zeros((OWN, start + SPAN - high), BF16)


def grad_kernel(counted, saved_ref, upstream_ref, sums_ref, params_ref, packed_ref, means_ref):
    saved_sum, square_sum, upstream_sum, product_sum = from_lanes(sums_ref, 4)
    mean = saved_sum / counted
    var = square_sum / counted - mean * mean
    inverse = lax.rsqrt(var + EPSILON)
    shift_grad = upstream_sum / counted
    gain_grad = (product_sum / counted - mean * shift_grad) * inverse
    means_ref[...] = in_lanes([gain_grad, shift_grad])
    scale = params_ref[2][:, :1] * inverse
    for block in range(NY):
        part = slice(block * BLOCK, (block + 1) * BLOCK)
        normed = (saved_ref[:, part].astype(F32) - mean) * inverse
        upstream = upstream_ref[:, part].astype(F32)
        grads = (scale * (upstream - shift_grad - normed * gain_grad)).astype(BF16)
        for to in range(NZ):
            packed_ref[block * NZ + to] = grads


def joined(parts_ref, block):
    whole = parts_ref[block, :, REACH : REACH + BLOCK].astype(F32)
    pieces = [whole[:, :384], whole[:, 384:REACH], whole[:, REACH:]]
    if block > 0:
        before = parts_ref[block - 1, :, REACH + BLOCK :].astype(F32)
        pieces[0] = pieces[0] + before[:, :384]
        pieces[1] = pieces[1] + before[:, 384:]
    if block < NY - 1:
        after = parts_ref[block + 1, :, :REACH].astype(F32)
        pieces[1] = pieces[1] + after[:, : REACH - 384]
        pieces[2] = pieces[2] + after[:, REACH - 384 :]
    return jnp.concatenate(pieces, axis=1)


def join_kernel(parts_ref, out_ref):
    for block in range(NY):
        out_ref[:, block * BLOCK : (block + 1) * BLOCK] = joined(parts_ref, block).astype(BF16)


def relu_kernel(counted, conv_ref, sums_ref, params_ref, out_ref):
    first_sum, square_sum = from_lanes(sums_ref, 2)
    mean = first_sum / counted
    var = square_sum / counted - mean * mean
    scale = params_ref[0][:, :1] * lax.rsqrt(var + EPSILON)
    bias = params_ref[1][:, :1]
    out_ref[...] = jnp.maximum((conv_ref[...] - mean) * scale + bias, 0.0).astype(BF16)


def shaped(shape, dtype):
    return jax.ShapeDtypeStruct(shape, dtype)


def call(kernel, outs, specs, scratch=()):
    return pl.pallas_call(
        kernel,
        out_shape=outs,
        in_specs=specs,
        out_specs=jax.tree.map(lambda _: VMEM, outs),
        scratch_shapes=list(scratch),
        compiler_params=PARAMS,
        cost_estimate=pl.CostEstimate(flops=1000, bytes_accessed=1000, transcendentals=0),
    )


def exchange(value, axes):
    return lax.all_to_all(value, axes, 0, 0, tiled=True)


def gathered(filters):
    filters = lax.all_gather(filters, "y", axis=0, tiled=False)
    return jnp.transpose(filters, (1, 0, 2, 3)).reshape(ROWS, CH)


def shards(
    fwd_input,
    weight_one,
    gain_one,
    bias_one,
    saved_conv,
    cotangent,
    saved_input,
    weight_two,
    gain_two,
):
    counted = lax.axis_size("vol") * CELLS
    base = (lax.axis_index("y") * BLOCK).astype(jnp.int32).reshape(1)
    params = jnp.broadcast_to(
        jnp.stack([gain_one, bias_one, gain_two])[:, :, None], (3, OWN, 128)
    )
    saved, upstream = saved_conv[0], cotangent[0]

    cells = lax.all_gather(fwd_input[0].T, ("y", "z"), axis=0, tiled=True)
    low = jnp.pad(weight_one, ((0, 0), (0, OWN), (0, 0))).reshape(27 * 2 * OWN, CH)
    high = jnp.pad(weight_one, ((0, 0), (OWN, 0), (0, 0))).reshape(27 * 2 * OWN, CH)

    sums_two = call(sums_kernel, shaped((OWN, 128), F32), [VMEM] * 2)(saved, upstream)
    acts = call(pack_kernel, shaped((NY, OWN, SPAN), BF16), [VMEM])(saved_input[0])
    acts = exchange(acts, "y")
    sums_two = lax.psum(sums_two, "vol")
    acts, sums_two = lax.optimization_barrier((acts, sums_two))
    acts = acts.reshape(GROUP, SPAN)
    packed, means = call(
        lambda *refs: grad_kernel(counted, *refs),
        (shaped((NY * NZ, OWN, BLOCK), BF16), shaped((OWN, 128), F32)),
        [VMEM] * 4,
    )(saved, upstream, sums_two, params)

    second, packed = lax.optimization_barrier((weight_two, packed))
    grads = exchange(packed, ("y", "z"))
    second = gathered(jnp.transpose(second, (0, 2, 1)))
    grads, second = lax.optimization_barrier((grads, second))
    grads = grads.reshape(CH, BLOCK)
    filter_parts = call(
        filter_kernel,
        shaped((8, NY, GROUP, 128), BF16),
        [SMEM, VMEM, VMEM],
        [pltpu.VMEM((1024, BLOCK), BF16), pltpu.VMEM((CH, 1024), BF16)],
    )(base, grads, acts)
    second, filter_parts = lax.optimization_barrier((second, filter_parts))
    filter_parts = exchange(filter_parts.reshape(8 * NY, GROUP, 128), ("vol", "y"))
    input_parts = call(
        backward_kernel,
        shaped((NY, OWN, SPAN), BF16),
        [SMEM, VMEM, VMEM],
        [pltpu.VMEM((ROWS, BLOCK), F32)],
    )(base, second, grads)

    cells, _ = lax.optimization_barrier((cells, (input_parts, filter_parts)))
    input_parts, _ = lax.optimization_barrier((input_parts, filter_parts))
    input_parts = exchange(input_parts, "y")
    conv_out, sums_one = pl.pallas_call(
        forward_kernel,
        out_shape=(shaped((OWN, CELLS), F32), shaped((OWN, 128), F32)),
        grid=(HALF,),
        in_specs=[
            pl.BlockSpec((27 * 2 * OWN, CH), lambda at: (0, 0)),
            pl.BlockSpec((27 * 2 * OWN, CH), lambda at: (0, 0)),
            pl.BlockSpec((PLANE, CH), lambda at: (at, 0)),
            pl.BlockSpec((PLANE, CH), lambda at: (at + HALF, 0)),
        ],
        out_specs=(
            pl.BlockSpec((OWN, CELLS), lambda at: (0, 0)),
            pl.BlockSpec((OWN, 128), lambda at: (0, 0)),
        ),
        scratch_shapes=[
            pltpu.VMEM((27 * 2 * OWN, PLANE), F32),
            pltpu.VMEM((2 * OWN, (HALF + 2) * PLANE), F32),
        ],
        compiler_params=PARAMS,
        cost_estimate=pl.CostEstimate(flops=1000, bytes_accessed=1000, transcendentals=0),
    )(low, high, cells, cells)
    sums_one = lax.psum(sums_one, "vol")
    activation = call(
        lambda *refs: relu_kernel(counted, *refs), shaped((OWN, CELLS), BF16), [VMEM] * 3
    )(conv_out, sums_one, params)
    input_grad = call(join_kernel, shaped((OWN, CELLS), BF16), [VMEM])(input_parts)

    summed = jnp.sum(filter_parts.astype(F32), axis=0) / math.sqrt(counted)
    weight_grad = jnp.transpose(summed[:, : 27 * OWN].reshape(GROUP, 27, OWN), (1, 0, 2))
    return (activation[None], input_grad[None], weight_grad, means[:, 0], means[:, 1])


def solution(mesh):
    cut = Mesh(mesh.devices.reshape(mesh.devices.shape[0], NY, NZ), ("vol", "y", "z"))
    chan = ("y", "z")
    return jax.shard_map(
        shards,
        mesh=cut,
        in_specs=(
            P("vol", None, chan),
            P(None, chan, None),
            P(chan),
            P(chan),
            P("vol", chan, None),
            P("vol", chan, None),
            P("vol", chan, None),
            P(None, None, chan),
            P(chan),
        ),
        out_specs=(
            P("vol", chan, None),
            P("vol", chan, None),
            P(None, "vol", chan),
            P(chan),
            P(chan),
        ),
        check_vma=False,
    )
```
